256 devices in a mesh: seq: 32 (over z, x), exp: 8 (over y, core).
Axes of the slice: x: 4, y: 4, z: 8, core: 2. Of those that a mesh axis runs over, the one named last changes fastest.
Arguments:
- mixer_input: bfloat16 [2048, 8192], P('seq', 'exp'), may hold values from -6 to 6
- gate_input: bfloat16 [2048, 8192], P('seq', 'exp'), may hold values from -6 to 6
- conv_weight: bfloat16 [4, 8192], P(None, 'exp'), may hold values from -3 to 3
- conv_bias: float32 [8192], P('exp'), may hold values from -3 to 3
- rank_weight: bfloat16 [8192, 256], P('exp'), may hold values from -0.0625 to 0.0625
- state_weight: bfloat16 [8192, 32], P('exp'), may hold values from -0.03125 to 0.03125
- delta_weight: bfloat16 [256, 8192], P(None, 'exp'), may hold values from -0.375 to 0.375
- delta_bias: float32 [8192], P('exp'), may hold values from -1 to 1
- log_rates: float32 [16, 8192], P(None, 'exp'), may hold values from -10 to -1
- skip_gain: float32 [8192], P('exp'), may hold values from 0.5 to 1.5
- out_proj: bfloat16 [8192, 4096], P('exp', 'seq'), may hold values from -0.0625 to 0.0625
- residual: bfloat16 [2048, 4096], P(('seq', 'exp')), may hold values from -3 to 3
- norm_gain: float32 [4096], replicated, may hold values from 0.5 to 1.5
- router: float32 [4096, 8], replicated, may hold values from -0.09375 to 0.09375
- w_gate: bfloat16 [8, 4096, 14336], P('exp', None, 'seq'), may hold values from -0.09375 to 0.09375
- w_up: bfloat16 [8, 4096, 14336], P('exp', None, 'seq'), may hold values from -0.09375 to 0.09375
- w_down: bfloat16 [8, 14336, 4096], P('exp', 'seq'), may hold values from -0.09375 to 0.09375
- routes: int32 [2048, 2], P(('seq', 'exp')), may hold values from 0 to 7, all different within a row; in each aligned block of 8 rows (0 to 7, 8 to 15, ...) at most 4 rows name the same one
Outputs:
- layer_out: bfloat16 [2048, 4096], P(('seq', 'exp'))
- expert_mix: float32 [2048, 4096], P(('seq', 'exp'))
The draws below stay inside these ranges and needn't reach their ends.
Inputs may be any that keep to these rules, and one draw needn't show every extreme that they name: `routes`: each row names two different experts; among the 8 rows of one device no expert is named more than 4 times, a bound that some block reaches there on some device.
All inputs are finite; a program needn't handle non-finite values.
Results may differ from the reference program's by a relative error of at most 0.024.
Values may be sent and summed in bfloat16 or wider, within the bound.
No kernel may reach another device: no remote copies, remote signals or barrier semaphores. Data moves between devices by JAX's collectives and lax.ppermute only.
A program may use at most 128 MiB of HBM per device.

```python
import math
import jax
import jax.numpy as jnp
import numpy as np
from jax import lax

D = 4096
INNER = 8192
STATE = 16
DT_RANK = 256
CONV = 4
FF = 14336
TOK_DEV = 8
SEQ_LEN = 2048
EXPERTS = 8
CAP = 4
SLOTS = 1024
N_SEQ = 32


def draw_log_rates(key, part):
    key_kind, key_slow, key_fast, key_extra = jax.random.split(key, 4)
    share = 0.5
    chain_level = -math.log(float(SEQ_LEN))
    slow_kind = jax.random.uniform(key_kind, (1, INNER), jnp.float32) < share
    slow_vals = chain_level + jax.random.uniform(key_slow, (STATE, INNER), jnp.float32, -1.2, 0.0)
    fast_vals = jax.random.uniform(key_fast, (STATE, INNER), jnp.float32, -3.5, -2.3)
    extra = jax.random.uniform(key_extra, (STATE, INNER), jnp.float32, 0.0, 0.7)
    return (jnp.where(slow_kind, slow_vals, fast_vals) + extra).astype(jnp.float32)


def shard_levels(rng, extent, cuts, smallest, largest):
    def one(dim, blocks):
        heights = jax.random.uniform(jax.random.fold_in(jax.random.fold_in(rng, 6), dim), (blocks,), jnp.float32, smallest / len(cuts), largest / len(cuts))
        return jnp.repeat(jnp.exp(heights), extent[dim] // blocks).reshape((-1,) + (1,) * (len(extent) - dim - 1))

    level = one(*cuts[0])
    for cut in cuts[1:]:
        level = level * one(*cut)
    return level


def deal_out(own_key, own, number, rows, number_of, top, reach, slope):
    order = jax.random.permutation(own_key, number_of)
    heavy_load, usual = portions_of(number_of, rows * top, reach, slope, True), portions_of(number_of, rows * top, reach, slope, False)
    places = jnp.arange(number_of)

    def named(tallies, rotation):
        used = int((tallies > 0).sum())
        fixed = max(1, used // 4)
        moved = fixed + (places - fixed + rotation * (used - fixed)) % max(1, number_of - fixed)
        return jnp.zeros((number_of,), jnp.int32).at[order[jnp.where(places < fixed, places, moved)]].set(jnp.asarray(tallies, jnp.int32))

    tallies = jnp.where(number % 4 == 0, named(heavy_load, number // 4), named(usual, number - number // 4 - 1))
    mixed = jax.random.permutation(jax.random.fold_in(own, 3), number_of)
    source_of, sink = mixed[0:number_of // 2 * 2:2], mixed[1:number_of // 2 * 2:2]
    slack = jnp.minimum(tallies[source_of] - 1, reach - tallies[sink]) // 2
    slack = jnp.where((source_of == order[0]) | (sink == order[0]) | (tallies[sink] == 0), 0, jnp.maximum(slack, 0))
    moved = jax.random.randint(jax.random.fold_in(own, 4), (number_of // 2,), 0, 1 << 20) % (slack + 1)
    tallies = tallies.at[source_of].add(-moved).at[sink].add(moved)
    items = jnp.searchsorted(jnp.cumsum(tallies), jnp.arange(rows * top), side="right").astype(jnp.int32)
    grid = items.reshape(top, rows).T
    grid = grid[jax.random.permutation(jax.random.fold_in(own, 1), rows)]
    rotation = jax.random.randint(jax.random.fold_in(own, 2), (rows, 1), 0, top)
    return jnp.take_along_axis(grid, (jnp.arange(top)[None, :] + rotation) % top, axis=1)


def portions_of(amount, total, reach, slope, full):
    portions = [(1 << 20) // math.isqrt(grade ** slope) + 1 for grade in range(1, amount + 1)]
    largest = reach if full else min(reach, max(-(-total // amount), total * portions[0] // sum(portions)))
    least = 1 if total - largest >= amount - 1 else 0
    holding, surplus = [largest] + [least] * (amount - 1), total - largest - least * (amount - 1)
    while surplus > 0:
        candidates = [i for i in range(1, amount) if holding[i] < largest] or [i for i in range(1, amount) if holding[i] < reach]
        mass, left = sum([portions[i] for i in candidates]), surplus
        for i in candidates:
            more = min(reach - holding[i], max(1, left * portions[i] // mass), surplus)
            holding[i] = holding[i] + more
            surplus = surplus - more
    return np.array(holding)


def noise(stream_key, shape, scale, reach, cuts=(), kind=jnp.bfloat16):
    entries = scale * jax.random.normal(stream_key, shape, jnp.float32)
    if cuts:
        entries = entries * shard_levels(stream_key, shape, cuts, -0.22, 0.18)
    return jnp.clip(entries, -reach, reach).astype(kind)


def setup_inputs(seed: int = 0) -> dict:
    key_of = jax.random.split(jax.random.key(seed), 19)
    mixer_input = noise(key_of[0], (SEQ_LEN, INNER), 1.0, 6.0, ((0, 32), (1, 8)))
    gate_input = noise(key_of[1], (SEQ_LEN, INNER), 1.0, 6.0, ((0, 32), (1, 8)))
    conv_weight = noise(key_of[2], (CONV, INNER), CONV ** -0.5, 3.0, ((1, 8),))
    conv_bias = noise(key_of[3], (INNER,), 0.5, 3.0, ((0, 8),), jnp.float32)
    rank_weight = noise(key_of[4], (INNER, DT_RANK), INNER ** -0.5, 0.0625, ((0, 8),))
    state_weight = noise(key_of[5], (INNER, 2 * STATE), (INNER * 4) ** -0.5, 0.03125, ((0, 8),))
    delta_weight = noise(key_of[6], (DT_RANK, INNER), DT_RANK ** -0.5, 0.375, ((1, 8),))
    delta_bias = jnp.clip(jax.random.uniform(key_of[7], (INNER,), jnp.float32, -1.0, 1.0) * shard_levels(key_of[7], (INNER,), ((0, 8),), -0.4, 0.0), -1.0, 1.0)
    log_rates = draw_log_rates(jax.random.fold_in(key_of[18], 71), 0)
    skip_gain = jnp.clip(0.5 + 1.0 * jax.random.uniform(key_of[9], (INNER,), jnp.float32) ** shard_levels(key_of[9], (INNER,), ((0, 8),), -0.2, 0.2), 0.5, 1.5)
    out_proj = noise(key_of[10], (INNER, D), INNER ** -0.5, 0.0625, ((0, 8), (1, 32)))
    residual = noise(key_of[11], (SEQ_LEN, D), 0.5, 3.0, ((0, 256),))
    norm_gain = jnp.clip(1.0 + 0.1 * jax.random.normal(key_of[12], (D,), jnp.float32), 0.5, 1.5)
    router = noise(key_of[13], (D, EXPERTS), D ** -0.5, 0.09375, (), jnp.float32)
    w_gate = noise(key_of[14], (EXPERTS, D, FF), D ** -0.5, 0.09375, ((0, 8), (2, 32)))
    w_up = noise(key_of[15], (EXPERTS, D, FF), D ** -0.5, 0.09375, ((0, 8), (2, 32)))
    w_down = noise(key_of[16], (EXPERTS, FF, D), (FF // 4) ** -0.5, 0.09375, ((0, 8), (1, 32)))
    routes_keys = jax.random.split(jax.random.fold_in(key_of[17], 1), SEQ_LEN // TOK_DEV)
    routes_turns = jax.random.permutation(jax.random.fold_in(key_of[17], 3), SEQ_LEN // TOK_DEV)
    routes = jax.vmap(lambda own, number: deal_out(jax.random.fold_in(key_of[17], 2), own, number, TOK_DEV, EXPERTS, 2, CAP, 2))(routes_keys, routes_turns).reshape((SEQ_LEN, 2))
    return dict(mixer_input=mixer_input, gate_input=gate_input, conv_weight=conv_weight, conv_bias=conv_bias, rank_weight=rank_weight, state_weight=state_weight, delta_weight=delta_weight, delta_bias=delta_bias, log_rates=log_rates, skip_gain=skip_gain, out_proj=out_proj, residual=residual, norm_gain=norm_gain, router=router, w_gate=w_gate, w_up=w_up, w_down=w_down, routes=routes)


def reference(mixer_input, gate_input, conv_weight, conv_bias, rank_weight, state_weight, delta_weight, delta_bias, log_rates, skip_gain, out_proj, residual, norm_gain, router, w_gate, w_up, w_down, routes):
    padded = jnp.concatenate([jnp.zeros((CONV - 1, INNER), jnp.bfloat16), mixer_input], axis=0)
    conv_sum = jnp.zeros((SEQ_LEN, INNER), jnp.float32) + conv_bias[None, :]
    for offset in range(CONV):
        conv_sum = conv_sum + conv_weight[offset].astype(jnp.float32)[None, :] * padded[offset:offset + SEQ_LEN].astype(jnp.float32)
    conv_act = jax.nn.silu(conv_sum).astype(jnp.bfloat16)
    delta_low = jnp.dot(conv_act, rank_weight, preferred_element_type=jnp.float32).astype(jnp.bfloat16)
    state_maps = jnp.dot(conv_act, state_weight, preferred_element_type=jnp.float32)
    input_map = state_maps[:, :STATE]
    output_map = state_maps[:, STATE:]
    delta = jax.nn.softplus(jnp.dot(delta_low, delta_weight, preferred_element_type=jnp.float32) + delta_bias[None, :])
    decay_rate = jnp.exp(log_rates)
    conv_float = conv_act.astype(jnp.float32)

    def advance(carried, inputs):
        delta_t, conv_t, input_t, output_t = inputs
        carried = jnp.exp(-delta_t[None, :] * decay_rate) * carried + (delta_t * conv_t)[None, :] * input_t[:, None]
        return (carried, lax.optimization_barrier(jnp.sum(output_t[:, None] * carried, axis=0)))
    final_state, scan_out = lax.scan(advance, jnp.zeros((STATE, INNER), jnp.float32), (delta, conv_float, input_map, output_map))
    scan_out = scan_out + skip_gain[None, :] * conv_float
    gated = (scan_out * jax.nn.silu(gate_input.astype(jnp.float32))).astype(jnp.bfloat16)
    mamba_out = jnp.dot(gated, out_proj, preferred_element_type=jnp.float32)
    hidden = residual.astype(jnp.float32) + mamba_out
    mean_square = lax.optimization_barrier(jnp.mean(hidden * hidden, axis=1, keepdims=True))
    normed = (hidden * lax.rsqrt(mean_square + 1e-05) * norm_gain[None, :]).astype(jnp.bfloat16)
    logits = jnp.dot(normed.astype(jnp.float32), router, precision=lax.Precision.HIGHEST)
    chosen = jnp.take_along_axis(logits, routes, axis=1)
    route_weights = jax.nn.sigmoid(chosen - chosen[:, ::-1]).reshape(-1)
    flat_ids = routes.reshape(-1)
    route_pos = jnp.arange(2 * SEQ_LEN, dtype=jnp.int32)
    group_size = FF // N_SEQ

    def per_expert(total_out, expert):
        sort_keys = jnp.where(flat_ids == expert, route_pos, 2 * SEQ_LEN).astype(jnp.int32)
        picked = jnp.sort(sort_keys)[:SLOTS]
        is_valid = picked < 2 * SEQ_LEN
        safe_pos = jnp.minimum(picked, 2 * SEQ_LEN - 1).astype(jnp.int32)
        token_rows = (safe_pos // 2).astype(jnp.int32)
        rows_in = jnp.take(normed, token_rows, axis=0)
        gate_part = jnp.dot(rows_in, w_gate[expert], preferred_element_type=jnp.float32)
        up_part = jnp.dot(rows_in, w_up[expert], preferred_element_type=jnp.float32)
        activated = (jax.nn.silu(gate_part) * up_part).astype(jnp.bfloat16)
        act_groups = activated.reshape(SLOTS, N_SEQ, group_size).transpose(1, 0, 2)
        down_groups = w_down[expert].reshape(N_SEQ, group_size, D)

        def add_group(running, group_pair):
            act_group, down_group = group_pair
            group_term = jnp.dot(act_group, down_group, preferred_element_type=jnp.float32).astype(jnp.bfloat16)
            group_term = lax.optimization_barrier(group_term)
            return (running + group_term.astype(jnp.float32), None)
        expert_out, unused = lax.scan(add_group, jnp.zeros((SLOTS, D), jnp.float32), (act_groups, down_groups))
        weight_col = jnp.where(is_valid, jnp.take(route_weights, safe_pos), 0.0)
        total_out = total_out.at[token_rows].add(weight_col[:, None] * expert_out)
        return (total_out, None)
    moe_sum, unused = lax.scan(per_expert, jnp.zeros((SEQ_LEN, D), jnp.float32), jnp.arange(EXPERTS, dtype=jnp.int32))
    return ((hidden + moe_sum).astype(jnp.bfloat16), moe_sum)
```

```python
import jax
import jax.numpy as jnp
from jax import lax
from jax.experimental import pallas as pl
from jax.experimental.pallas import tpu as pltpu
from jax.sharding import PartitionSpec as P

NX = 4
LANES = 128
F32 = jnp.float32
BF16 = jnp.bfloat16


def seq_sizes():
    count = lax.axis_size("seq")
    return count // NX, NX


def groups_x():
    nz, nx = seq_sizes()
    return [[z * nx + x for x in range(nx)] for z in range(nz)]


def groups_z():
    nz, nx = seq_sizes()
    return [[z * nx + x for z in range(nz)] for x in range(nx)]


def send_z(block, step):
    nz, nx = seq_sizes()
    route = [
        (z * nx + x, ((z + step) % nz) * nx + x) for z in range(nz) for x in range(nx)
    ]
    return lax.ppermute(block, "seq", route)


def send_x(block, step):
    nz, nx = seq_sizes()
    route = [(z * nx + x, z * nx + (x + step) % nx) for z in range(nz) for x in range(nx)]
    return lax.ppermute(block, "seq", route)


def gather_x(block):
    return [block, send_x(block, -1), send_x(block, 2), send_x(block, 1)]


def gather_z(block):
    half = block.shape[0] // 2
    before1, after1 = send_z(block, 1), send_z(block, -1)
    before2, after2 = send_z(before1, 1), send_z(after1, -1)
    before3, after3 = send_z(before2, 1), send_z(after2, -1)
    far = [send_z(before3[:half], 1), send_z(after3[half:], -1)]
    return [block, after1, after2, after3, jnp.concatenate(far), before3, before2, before1]


def added(a, b):
    return (a.astype(F32) + b.astype(F32)).astype(BF16)


def scatter_z(parts):
    half = parts[0].shape[0] // 2
    up = send_z(parts[4][:half], 1)
    down = send_z(parts[4][half:], -1)
    up = send_z(jnp.concatenate([added(parts[3][:half], up), parts[3][half:]]), 1)
    down = send_z(jnp.concatenate([parts[5][:half], added(parts[5][half:], down)]), -1)
    up = send_z(added(parts[2], up), 1)
    down = send_z(added(parts[6], down), -1)
    up = send_z(added(parts[1], up), 1)
    down = send_z(added(parts[7], down), -1)
    return parts[0].astype(F32) + up.astype(F32) + down.astype(F32)


def scatter_x(parts):
    came = [send_x(parts[1], 1), send_x(parts[2], 2), send_x(parts[3], -1)]
    total = parts[0].astype(F32)
    for part in came:
        total = total + part.astype(F32)
    return total


def scan_kernel(
    low_ref, weight_ref, bias_ref, rates_ref, act_ref, maps_ref, out_ref, passed_ref, ends_ref,
    delta_ref, driven_ref,
):
    rows, width = act_ref.shape
    states = rates_ref.shape[0]
    tiles = width // LANES
    raw = jnp.dot(low_ref[...], weight_ref[...], preferred_element_type=F32) + bias_ref[...]
    delta = jnp.maximum(raw, 0.0) + jnp.log1p(jnp.exp(-jnp.abs(raw)))
    delta_ref[...] = delta
    driven_ref[...] = delta * act_ref[...].astype(F32)
    rate = -jnp.exp(rates_ref[...])

    def step(t, carry):
        state, passed = carry
        delta_t = delta_ref[pl.ds(t, 1), :]
        driven_t = driven_ref[pl.ds(t, 1), :]
        maps_t = maps_ref[t]
        input_t = jnp.concatenate([maps_t[:states]] * tiles, axis=1)
        output_t = jnp.concatenate([maps_t[states:]] * tiles, axis=1)
        state = jnp.exp(delta_t * rate) * state + driven_t * input_t
        passed = passed + delta_t
        out_ref[pl.ds(t, 1), :] = jnp.sum(output_t * state, axis=0, keepdims=True)
        passed_ref[pl.ds(t, 1), :] = passed
        return state, passed

    state, passed = lax.fori_loop(
        0, rows, step, (jnp.zeros((states, width), F32), jnp.zeros((1, width), F32)), unroll=4
    )
    ends_ref[:states, :] = state
    ends_ref[states:, :] = passed


def finish_kernel(
    local_ref, passed_ref, start_ref, rates_ref, maps_ref, act_ref, skip_ref, gate_ref, gated_ref,
    full_ref,
):
    rows, width = act_ref.shape
    states = rates_ref.shape[0]
    tiles = width // LANES
    rate = -jnp.exp(rates_ref[...])
    start = start_ref[...]

    def step(t, carry):
        left = jnp.exp(passed_ref[pl.ds(t, 1), :] * rate) * start
        output_t = jnp.concatenate([maps_ref[t][states:]] * tiles, axis=1)
        full_ref[pl.ds(t, 1), :] = local_ref[pl.ds(t, 1), :] + jnp.sum(
            output_t * left, axis=0, keepdims=True
        )
        return carry

    lax.fori_loop(0, rows, step, 0, unroll=4)
    gate = gate_ref[...].astype(F32)
    scan_out = full_ref[...] + skip_ref[...] * act_ref[...].astype(F32)
    gated_ref[...] = (scan_out * (gate / (1.0 + jnp.exp(-gate)))).astype(BF16)


VMEM = pl.BlockSpec(memory_space=pltpu.VMEM)


def local_scan(low, weight, bias, rates, act, maps):
    rows, width = act.shape
    return pl.pallas_call(
        scan_kernel,
        out_shape=(
            jax.ShapeDtypeStruct((rows, width), F32),
            jax.ShapeDtypeStruct((rows, width), F32),
            jax.ShapeDtypeStruct((rates.shape[0] + 1, width), F32),
        ),
        in_specs=[VMEM] * 6,
        out_specs=(VMEM,) * 3,
        scratch_shapes=[pltpu.VMEM((rows, width), F32), pltpu.VMEM((rows, width), F32)],
        compiler_params=pltpu.CompilerParams(vmem_limit_bytes=16 * 2**20),
    )(low, weight, bias, rates, act, maps)


def finish_scan(local, passed, start, rates, maps, act, skip, gate):
    rows, width = act.shape
    return pl.pallas_call(
        finish_kernel,
        out_shape=jax.ShapeDtypeStruct((rows, width), BF16),
        in_specs=[VMEM] * 8,
        out_specs=VMEM,
        scratch_shapes=[pltpu.VMEM((rows, width), F32)],
        compiler_params=pltpu.CompilerParams(vmem_limit_bytes=16 * 2**20),
    )(local, passed, start, rates, maps, act, skip, gate)


def exchanged(block, group):
    count = len(group[0])
    copies = jnp.broadcast_to(block[None], (count, *block.shape))
    return lax.all_to_all(copies, "seq", split_axis=0, concat_axis=0, axis_index_groups=group)


def prefix(blocks, rate, limit):
    states = rate.shape[0]
    state = jnp.zeros(rate.shape, F32)
    passed = jnp.zeros((1, rate.shape[1]), F32)
    for k in range(blocks.shape[0]):
        block = blocks[k]
        took = block[states:]
        reached = k < limit
        state = jnp.where(reached, jnp.exp(-took * rate) * state + block[:states], state)
        passed = jnp.where(reached, passed + took, passed)
    return state, passed


def mixer(
    mixer_input, gate_input, conv_weight, conv_bias, rank_weight, state_weight, delta_weight,
    delta_bias, log_rates, skip_gain, out_proj,
):
    taps = conv_weight.shape[0]
    block_rows = mixer_input.shape[0]
    nz, nx = seq_sizes()
    experts = lax.axis_size("exp")
    columns = lax.all_gather(
        out_proj, "seq", axis=1, tiled=True, axis_index_groups=groups_z()
    )
    rim_rows = lax.ppermute(
        mixer_input[block_rows - (taps - 1) :], "seq", [(i, i + 1) for i in range(nz * nx - 1)]
    )
    before = jnp.concatenate([rim_rows, mixer_input], axis=0)
    conv_sum = jnp.zeros(mixer_input.shape, F32) + conv_bias[None, :]
    for offset in range(taps):
        conv_sum = conv_sum + conv_weight[offset].astype(F32)[None, :] * before[
            offset : offset + block_rows
        ].astype(F32)
    conv_act = jax.nn.silu(conv_sum).astype(BF16)
    both = jnp.concatenate([rank_weight, state_weight], axis=1)
    sums = jnp.dot(conv_act, both, preferred_element_type=F32)
    rank = rank_weight.shape[1]
    coarse = lax.reduce_precision(sums, 8, 7)
    fine = sums[:, rank:] - coarse[:, rank:]
    sent = jnp.concatenate([coarse, fine], axis=1).astype(BF16)
    summed = jnp.sum(lax.all_gather(sent, "exp").astype(F32), axis=0)
    maps = summed[:, rank : sums.shape[1]] + summed[:, sums.shape[1] :]
    delta_low = summed[:, :rank].astype(BF16)
    wide_maps = jnp.broadcast_to(maps[:, :, None], (*maps.shape, LANES))
    local, passed, ends = local_scan(
        delta_low, delta_weight, delta_bias[None], log_rates, conv_act, wide_maps
    )
    rate = jnp.exp(log_rates)
    z, x = lax.axis_index("seq") // nx, lax.axis_index("seq") % nx
    along_x = exchanged(ends, groups_x())
    row_start, row_passed = prefix(along_x, rate, x)
    along_z = exchanged(jnp.concatenate(prefix(along_x, rate, nx)), groups_z())
    start = jnp.exp(-row_passed * rate) * prefix(along_z, rate, z)[0] + row_start
    gated = finish_scan(
        local, passed, start, log_rates, wide_maps, conv_act, skip_gain[None], gate_input
    )
    gated_row = lax.all_gather(gated, "seq", axis=0, tiled=True, axis_index_groups=groups_x())
    partial_value = jnp.dot(gated_row, columns, preferred_element_type=F32).astype(BF16)
    planes = [
        [(k * nx + i) * experts + e for i in range(nx) for e in range(experts)] for k in range(nz)
    ]
    came = lax.all_to_all(
        partial_value, ("seq", "exp"), split_axis=0, concat_axis=0, tiled=True,
        axis_index_groups=planes,
    )
    own_rows = block_rows // experts
    came = came.reshape(nx, experts, own_rows, nz, -1).astype(F32)
    return jnp.sum(came, axis=1).transpose(1, 2, 0, 3).reshape(own_rows, -1)


def body(
    mixer_input,
    gate_input,
    conv_weight,
    conv_bias,
    rank_weight,
    state_weight,
    delta_weight,
    delta_bias,
    log_rates,
    skip_gain,
    out_proj,
    residual,
    norm_gain,
    router,
    w_gate,
    w_up,
    w_down,
    routes,
):
    mamba_out = mixer(
        mixer_input, gate_input, conv_weight, conv_bias, rank_weight, state_weight,
        delta_weight, delta_bias, log_rates, skip_gain, out_proj,
    )
    tok_dev = residual.shape[0]
    hidden = residual.astype(F32) + mamba_out
    mean_square = jnp.mean(hidden * hidden, axis=1, keepdims=True)
    normed = (hidden * lax.rsqrt(mean_square + 1e-05) * norm_gain[None, :]).astype(BF16)
    logits = jnp.dot(normed.astype(F32), router, precision=lax.Precision.HIGHEST)
    experts = router.shape[1]
    expert_ids = jnp.arange(experts, dtype=jnp.int32)
    matches = (routes[:, :, None] == expert_ids[None, None, :]).astype(F32)
    chosen = jnp.sum(matches * logits[:, None, :], axis=2)
    route_weights = jax.nn.sigmoid(chosen - chosen[:, ::-1])
    capacity = max(2, 4 * tok_dev // experts)
    flat_ids = routes.reshape(-1)
    route_pos = jnp.arange(flat_ids.shape[0], dtype=jnp.int32)
    earlier_same = (flat_ids[:, None] == flat_ids[None, :]) & (
        route_pos[None, :] < route_pos[:, None]
    )
    slot_rank = jnp.sum(earlier_same.astype(jnp.int32), axis=1)
    slot_of = (flat_ids * capacity + slot_rank).reshape(tok_dev, 2)
    slot_ids = jnp.arange(experts * capacity, dtype=jnp.int32)
    taken = slot_of[:, :, None] == slot_ids[None, None, :]
    placing = jnp.sum(taken.astype(F32), axis=1).astype(BF16)
    outbound = lax.dot_general(
        placing, normed, (((0,), (0,)), ((), ())), preferred_element_type=F32
    ).astype(BF16)
    arrived = lax.all_to_all(outbound, "exp", split_axis=0, concat_axis=0, tiled=True)
    gate_local, up_local, down_local = w_gate[0], w_up[0], w_down[0]

    def expert(rows):
        gate_part = jnp.dot(rows, gate_local, preferred_element_type=F32)
        up_part = jnp.dot(rows, up_local, preferred_element_type=F32)
        activated = (jax.nn.silu(gate_part) * up_part).astype(BF16)
        return jnp.dot(activated, down_local, preferred_element_type=F32).astype(BF16)

    def expert_list(blocks):
        size = blocks[0].shape[0]
        out = expert(jnp.concatenate(blocks))
        return [out[k * size : (k + 1) * size] for k in range(len(blocks))]

    half = arrived.shape[0] // 2
    first, second = arrived[:half], arrived[half:]
    quads = gather_z(jnp.concatenate(gather_x(first)))
    lines = gather_z(second)
    near_order, far_order = (0, 1, 7, 2), (6, 3, 5, 4)
    near = gather_x(jnp.concatenate([lines[d] for d in near_order]))
    far = gather_x(jnp.concatenate([lines[d] for d in far_order]))

    near_out = expert_list(near)
    near_sum = scatter_x(near_out)
    quad_out = dict(zip((0, 1, 7, 2, 6), expert_list([quads[d] for d in (0, 1, 7, 2, 6)])))
    quad_out.update(zip((3, 5, 4), expert_list([quads[d] for d in (3, 5, 4)])))
    far_out = expert_list(far)
    far_sum = scatter_x(far_out)
    quad_sum = scatter_z([quad_out[d] for d in range(8)]).astype(BF16)
    first_sum = scatter_x([quad_sum[k * half : (k + 1) * half] for k in range(NX)])
    line_sum = {}
    for order, total in ((near_order, near_sum), (far_order, far_sum)):
        for k, d in enumerate(order):
            line_sum[d] = total[k * half : (k + 1) * half].astype(BF16)
    second_sum = scatter_z([line_sum[d] for d in range(8)])

    expert_out = jnp.concatenate([first_sum, second_sum]).astype(BF16)
    returned = lax.all_to_all(expert_out, "exp", split_axis=0, concat_axis=0, tiled=True)
    mixing = jnp.sum(taken.astype(F32) * route_weights[:, :, None], axis=1)
    moe_sum = jnp.dot(mixing, returned.astype(F32), precision=lax.Precision.HIGHEST)
    return ((hidden + moe_sum).astype(BF16), moe_sum)


def solution(mesh):
    in_specs = (
        P("seq", "exp"),
        P("seq", "exp"),
        P(None, "exp"),
        P("exp"),
        P("exp", None),
        P("exp", None),
        P(None, "exp"),
        P("exp"),
        P(None, "exp"),
        P("exp"),
        P("exp", "seq"),
        P(("seq", "exp"), None),
        P(),
        P(),
        P("exp", None, "seq"),
        P("exp", None, "seq"),
        P("exp", "seq", None),
        P(("seq", "exp"), None),
    )
    out_specs = (P(("seq", "exp"), None), P(("seq", "exp"), None))
    return jax.shard_map(body, mesh=mesh, in_specs=in_specs, out_specs=out_specs, check_vma=False)
```

```python
import jax
import jax.numpy as jnp
from jax import lax
from jax.experimental import pallas as pl
from jax.experimental.pallas import tpu as pltpu
from jax.sharding import PartitionSpec as P

NX = 4
LANES = 128
F32 = jnp.float32
BF16 = jnp.bfloat16


def seq_sizes():
    count = lax.axis_size("seq")
    return count // NX, NX


def groups_x():
    nz, nx = seq_sizes()
    return [[z * nx + x for x in range(nx)] for z in range(nz)]


def groups_z():
    nz, nx = seq_sizes()
    return [[z * nx + x for z in range(nz)] for x in range(nx)]


def send_z(block, step):
    nz, nx = seq_sizes()
    route = [
        (z * nx + x, ((z + step) % nz) * nx + x) for z in range(nz) for x in range(nx)
    ]
    return lax.ppermute(block, "seq", route)


def send_x(block, step):
    nz, nx = seq_sizes()
    route = [(z * nx + x, z * nx + (x + step) % nx) for z in range(nz) for x in range(nx)]
    return lax.ppermute(block, "seq", route)


def gather_x(block):
    return [block, send_x(block, -1), send_x(block, 2), send_x(block, 1)]


def gather_z(block):
    half = block.shape[0] // 2
    before1, after1 = send_z(block, 1), send_z(block, -1)
    before2, after2 = send_z(before1, 1), send_z(after1, -1)
    before3, after3 = send_z(before2, 1), send_z(after2, -1)
    far = [send_z(before3[:half], 1), send_z(after3[half:], -1)]
    return [block, after1, after2, after3, jnp.concatenate(far), before3, before2, before1]


def added(a, b):
    return (a.astype(F32) + b.astype(F32)).astype(BF16)


def scatter_z(parts):
    half = parts[0].shape[0] // 2
    up = send_z(parts[4][:half], 1)
    down = send_z(parts[4][half:], -1)
    up = send_z(jnp.concatenate([added(parts[3][:half], up), parts[3][half:]]), 1)
    down = send_z(jnp.concatenate([parts[5][:half], added(parts[5][half:], down)]), -1)
    up = send_z(added(parts[2], up), 1)
    down = send_z(added(parts[6], down), -1)
    up = send_z(added(parts[1], up), 1)
    down = send_z(added(parts[7], down), -1)
    return parts[0].astype(F32) + up.astype(F32) + down.astype(F32)


def scatter_x(parts):
    came = [send_x(parts[1], 1), send_x(parts[2], 2), send_x(parts[3], -1)]
    total = parts[0].astype(F32)
    for part in came:
        total = total + part.astype(F32)
    return total


def scan_kernel(
    low_ref, weight_ref, bias_ref, rates_ref, act_ref, maps_ref, out_ref, passed_ref, ends_ref,
    delta_ref, driven_ref,
):
    rows, width = act_ref.shape
    states = rates_ref.shape[0]
    tiles = width // LANES
    raw = jnp.dot(low_ref[...], weight_ref[...], preferred_element_type=F32) + bias_ref[...]
    delta = jnp.maximum(raw, 0.0) + jnp.log1p(jnp.exp(-jnp.abs(raw)))
    delta_ref[...] = delta
    driven_ref[...] = delta * act_ref[...].astype(F32)
    rate = -jnp.exp(rates_ref[...])

    def step(t, carry):
        state, passed = carry
        delta_t = delta_ref[pl.ds(t, 1), :]
        driven_t = driven_ref[pl.ds(t, 1), :]
        maps_t = maps_ref[t]
        input_t = jnp.concatenate([maps_t[:states]] * tiles, axis=1)
        output_t = jnp.concatenate([maps_t[states:]] * tiles, axis=1)
        state = jnp.exp(delta_t * rate) * state + driven_t * input_t
        passed = passed + delta_t
        out_ref[pl.ds(t, 1), :] = jnp.sum(output_t * state, axis=0, keepdims=True)
        passed_ref[pl.ds(t, 1), :] = passed
        return state, passed

    state, passed = lax.fori_loop(
        0, rows, step, (jnp.zeros((states, width), F32), jnp.zeros((1, width), F32)), unroll=4
    )
    ends_ref[:states, :] = state
    ends_ref[states:, :] = passed


def finish_kernel(
    local_ref, passed_ref, start_ref, rates_ref, maps_ref, act_ref, skip_ref, gate_ref, gated_ref,
    full_ref,
):
    rows, width = act_ref.shape
    states = rates_ref.shape[0]
    tiles = width // LANES
    rate = -jnp.exp(rates_ref[...])
    start = start_ref[...]

    def step(t, carry):
        left = jnp.exp(passed_ref[pl.ds(t, 1), :] * rate) * start
        output_t = jnp.concatenate([maps_ref[t][states:]] * tiles, axis=1)
        full_ref[pl.ds(t, 1), :] = local_ref[pl.ds(t, 1), :] + jnp.sum(
            output_t * left, axis=0, keepdims=True
        )
        return carry

    lax.fori_loop(0, rows, step, 0, unroll=4)
    gate = gate_ref[...].astype(F32)
    scan_out = full_ref[...] + skip_ref[...] * act_ref[...].astype(F32)
    gated_ref[...] = (scan_out * (gate / (1.0 + jnp.exp(-gate)))).astype(BF16)


VMEM = pl.BlockSpec(memory_space=pltpu.VMEM)


def local_scan(low, weight, bias, rates, act, maps):
    rows, width = act.shape
    return pl.pallas_call(
        scan_kernel,
        out_shape=(
            jax.ShapeDtypeStruct((rows, width), F32),
            jax.ShapeDtypeStruct((rows, width), F32),
            jax.ShapeDtypeStruct((rates.shape[0] + 1, width), F32),
        ),
        in_specs=[VMEM] * 6,
        out_specs=(VMEM,) * 3,
        scratch_shapes=[pltpu.VMEM((rows, width), F32), pltpu.VMEM((rows, width), F32)],
        compiler_params=pltpu.CompilerParams(vmem_limit_bytes=16 * 2**20),
    )(low, weight, bias, rates, act, maps)


def finish_scan(local, passed, start, rates, maps, act, skip, gate):
    rows, width = act.shape
    return pl.pallas_call(
        finish_kernel,
        out_shape=jax.ShapeDtypeStruct((rows, width), BF16),
        in_specs=[VMEM] * 8,
        out_specs=VMEM,
        scratch_shapes=[pltpu.VMEM((rows, width), F32)],
        compiler_params=pltpu.CompilerParams(vmem_limit_bytes=16 * 2**20),
    )(local, passed, start, rates, maps, act, skip, gate)


def expert_kernel(count, steps, *refs):
    rows = refs[:count]
    gate_ref, up_ref, down_ref = refs[count : count + 3]
    outs = refs[count + 3 : 2 * count + 3]
    gate_sum, up_sum, act_ref = refs[2 * count + 3 :]
    size = rows[0].shape[0]
    i = pl.program_id(0)

    @pl.when(i < steps)
    def _():
        taken = jnp.concatenate([r[...] for r in rows], axis=0)
        gate = jnp.dot(taken, gate_ref[...], preferred_element_type=F32)
        up = jnp.dot(taken, up_ref[...], preferred_element_type=F32)

        @pl.when(i == 0)
        def _():
            gate_sum[...] = gate
            up_sum[...] = up

        @pl.when(i > 0)
        def _():
            gate_sum[...] += gate
            up_sum[...] += up

    @pl.when(i >= steps)
    def _():
        @pl.when(i == steps)
        def _():
            gate = gate_sum[...]
            act_ref[...] = (gate / (1.0 + jnp.exp(-gate)) * up_sum[...]).astype(BF16)

        out = jnp.dot(act_ref[...], down_ref[...], preferred_element_type=F32).astype(BF16)
        for k in range(count):
            outs[k][...] = out[k * size : (k + 1) * size]


def experts_of(blocks, gate_local, up_local, down_local):
    count = len(blocks)
    size, features = blocks[0].shape
    hidden = gate_local.shape[1]
    steps = 4
    width = features // steps
    early = lambda i: jnp.minimum(i, steps - 1)
    late = lambda i: jnp.maximum(i - steps, 0)
    flops = 6 * count * size * features * hidden
    moved = 6 * features * hidden + 4 * count * size * features
    return pl.pallas_call(
        lambda *refs: expert_kernel(count, steps, *refs),
        grid=(2 * steps,),
        out_shape=[jax.ShapeDtypeStruct((size, features), BF16)] * count,
        in_specs=[pl.BlockSpec((size, width), lambda i: (0, early(i)))] * count
        + [pl.BlockSpec((width, hidden), lambda i: (early(i), 0))] * 2
        + [pl.BlockSpec((hidden, width), lambda i: (0, late(i)))],
        out_specs=[pl.BlockSpec((size, width), lambda i: (0, late(i)))] * count,
        scratch_shapes=[
            pltpu.VMEM((count * size, hidden), F32),
            pltpu.VMEM((count * size, hidden), F32),
            pltpu.VMEM((count * size, hidden), BF16),
        ],
        cost_estimate=pl.CostEstimate(
            flops=flops, bytes_accessed=moved, transcendentals=count * size * hidden
        ),
        compiler_params=pltpu.CompilerParams(vmem_limit_bytes=24 * 2**20),
    )(*blocks, gate_local, up_local, down_local)


def exchanged(blocks, group):
    return lax.all_to_all(
        blocks, "seq", split_axis=0, concat_axis=0, tiled=True, axis_index_groups=group
    )


def after(ends, took, state, rate):
    return jnp.exp(-took * rate) * state + ends


def entering(ends, log_rates):
    nz, nx = seq_sizes()
    states, width = log_rates.shape
    share = width // nx
    z, x = lax.axis_index("seq") // nx, lax.axis_index("seq") % nx
    rate = jnp.exp(lax.dynamic_slice_in_dim(log_rates, x * share, share, axis=1))
    shares = ends.reshape(states + 1, nx, share).transpose(1, 0, 2)
    row = exchanged(shares, groups_x())
    state, took = jnp.zeros(rate.shape, F32), jnp.zeros((1, share), F32)
    for k in range(nx):
        state = after(row[k, :states], row[k, states:], state, rate)
        took = took + row[k, states:]
    total = jnp.concatenate([state, took])
    rows = exchanged(jnp.broadcast_to(total[None], (nz, *total.shape)), groups_z())
    state = jnp.zeros(rate.shape, F32)
    for k in range(nz - 1):
        state = jnp.where(k < z, after(rows[k, :states], rows[k, states:], state, rate), state)
    starts = [state]
    for k in range(nx - 1):
        starts.append(after(row[k, :states], row[k, states:], starts[-1], rate))
    return exchanged(jnp.stack(starts), groups_x()).transpose(1, 0, 2).reshape(states, width)


def mixer(
    mixer_input, gate_input, conv_weight, conv_bias, rank_weight, state_weight, delta_weight,
    delta_bias, log_rates, skip_gain, out_proj,
):
    taps = conv_weight.shape[0]
    block_rows = mixer_input.shape[0]
    nz, nx = seq_sizes()
    experts = lax.axis_size("exp")
    columns = lax.all_gather(
        out_proj, "seq", axis=1, tiled=True, axis_index_groups=groups_z()
    )
    rim_rows = lax.ppermute(
        mixer_input[block_rows - (taps - 1) :], "seq", [(i, i + 1) for i in range(nz * nx - 1)]
    )
    before = jnp.concatenate([rim_rows, mixer_input], axis=0)
    conv_sum = jnp.zeros(mixer_input.shape, F32) + conv_bias[None, :]
    for offset in range(taps):
        conv_sum = conv_sum + conv_weight[offset].astype(F32)[None, :] * before[
            offset : offset + block_rows
        ].astype(F32)
    conv_act = jax.nn.silu(conv_sum).astype(BF16)
    both = jnp.concatenate([rank_weight, state_weight], axis=1)
    sums = jnp.dot(conv_act, both, preferred_element_type=F32)
    rank = rank_weight.shape[1]
    coarse = lax.reduce_precision(sums, 8, 7)
    fine = sums[:, rank:] - coarse[:, rank:]
    sent = jnp.concatenate([coarse, fine], axis=1).astype(BF16)
    summed = jnp.sum(lax.all_gather(sent, "exp").astype(F32), axis=0)
    maps = summed[:, rank : sums.shape[1]] + summed[:, sums.shape[1] :]
    delta_low = summed[:, :rank].astype(BF16)
    wide_maps = jnp.broadcast_to(maps[:, :, None], (*maps.shape, LANES))
    local, passed, ends = local_scan(
        delta_low, delta_weight, delta_bias[None], log_rates, conv_act, wide_maps
    )
    start = entering(ends, log_rates)
    gated = finish_scan(
        local, passed, start, log_rates, wide_maps, conv_act, skip_gain[None], gate_input
    )
    gated_row = lax.all_gather(gated, "seq", axis=0, tiled=True, axis_index_groups=groups_x())
    partial_value = jnp.dot(gated_row, columns, preferred_element_type=F32).astype(BF16)
    planes = [
        [(k * nx + i) * experts + e for i in range(nx) for e in range(experts)] for k in range(nz)
    ]
    came = lax.all_to_all(
        partial_value, ("seq", "exp"), split_axis=0, concat_axis=0, tiled=True,
        axis_index_groups=planes,
    )
    own_rows = block_rows // experts
    came = came.reshape(nx, experts, own_rows, nz, -1).astype(F32)
    return jnp.sum(came, axis=1).transpose(1, 2, 0, 3).reshape(own_rows, -1)


def body(
    mixer_input,
    gate_input,
    conv_weight,
    conv_bias,
    rank_weight,
    state_weight,
    delta_weight,
    delta_bias,
    log_rates,
    skip_gain,
    out_proj,
    residual,
    norm_gain,
    router,
    w_gate,
    w_up,
    w_down,
    routes,
):
    mamba_out = mixer(
        mixer_input, gate_input, conv_weight, conv_bias, rank_weight, state_weight,
        delta_weight, delta_bias, log_rates, skip_gain, out_proj,
    )
    tok_dev = residual.shape[0]
    hidden = residual.astype(F32) + mamba_out
    mean_square = jnp.mean(hidden * hidden, axis=1, keepdims=True)
    normed = (hidden * lax.rsqrt(mean_square + 1e-05) * norm_gain[None, :]).astype(BF16)
    logits = jnp.dot(normed.astype(F32), router, precision=lax.Precision.HIGHEST)
    experts = router.shape[1]
    expert_ids = jnp.arange(experts, dtype=jnp.int32)
    matches = (routes[:, :, None] == expert_ids[None, None, :]).astype(F32)
    chosen = jnp.sum(matches * logits[:, None, :], axis=2)
    route_weights = jax.nn.sigmoid(chosen - chosen[:, ::-1])
    capacity = max(2, 4 * tok_dev // experts)
    flat_ids = routes.reshape(-1)
    route_pos = jnp.arange(flat_ids.shape[0], dtype=jnp.int32)
    earlier_same = (flat_ids[:, None] == flat_ids[None, :]) & (
        route_pos[None, :] < route_pos[:, None]
    )
    slot_rank = jnp.sum(earlier_same.astype(jnp.int32), axis=1)
    slot_of = (flat_ids * capacity + slot_rank).reshape(tok_dev, 2)
    slot_ids = jnp.arange(experts * capacity, dtype=jnp.int32)
    taken = slot_of[:, :, None] == slot_ids[None, None, :]
    placing = jnp.sum(taken.astype(F32), axis=1).astype(BF16)
    outbound = lax.dot_general(
        placing, normed, (((0,), (0,)), ((), ())), preferred_element_type=F32
    ).astype(BF16)
    arrived = lax.all_to_all(outbound, "exp", split_axis=0, concat_axis=0, tiled=True)
    gate_local, up_local, down_local = w_gate[0], w_up[0], w_down[0]

    def expert_list(blocks):
        return experts_of(blocks, gate_local, up_local, down_local)

    half = arrived.shape[0] // 2
    first, second = arrived[:half], arrived[half:]
    lines = gather_z(second)
    row = jnp.concatenate(gather_x(first))
    row, lines[2], lines[6] = lax.optimization_barrier((row, lines[2], lines[6]))
    quads = gather_z(row)
    near_order, far_order = (0, 1, 7, 2), (6, 3, 5, 4)
    near = gather_x(jnp.concatenate([lines[d] for d in near_order]))
    far = gather_x(jnp.concatenate([lines[d] for d in far_order]))

    near_out = expert_list(near)
    near_out, far = lax.optimization_barrier((near_out, far))
    near_sum = scatter_x(near_out)
    quad_out = dict(zip((0, 1, 7, 2, 6), expert_list([quads[d] for d in (0, 1, 7, 2, 6)])))
    quad_out.update(zip((3, 5, 4), expert_list([quads[d] for d in (3, 5, 4)])))
    far_out = expert_list(far)
    far_sum = scatter_x(far_out)
    quad_sum = scatter_z([quad_out[d] for d in range(8)]).astype(BF16)
    first_sum = scatter_x([quad_sum[k * half : (k + 1) * half] for k in range(NX)])
    line_sum = {}
    for order, total in ((near_order, near_sum), (far_order, far_sum)):
        for k, d in enumerate(order):
            line_sum[d] = total[k * half : (k + 1) * half].astype(BF16)
    second_sum = scatter_z([line_sum[d] for d in range(8)])

    expert_out = jnp.concatenate([first_sum, second_sum]).astype(BF16)
    returned = lax.all_to_all(expert_out, "exp", split_axis=0, concat_axis=0, tiled=True)
    mixing = jnp.sum(taken.astype(F32) * route_weights[:, :, None], axis=1)
    moe_sum = jnp.dot(mixing, returned.astype(F32), precision=lax.Precision.HIGHEST)
    return ((hidden + moe_sum).astype(BF16), moe_sum)


def solution(mesh):
    in_specs = (
        P("seq", "exp"),
        P("seq", "exp"),
        P(None, "exp"),
        P("exp"),
        P("exp", None),
        P("exp", None),
        P(None, "exp"),
        P("exp"),
        P(None, "exp"),
        P("exp"),
        P("exp", "seq"),
        P(("seq", "exp"), None),
        P(),
        P(),
        P("exp", None, "seq"),
        P("exp", None, "seq"),
        P("exp", "seq", None),
        P(("seq", "exp"), None),
    )
    out_specs = (P(("seq", "exp"), None), P(("seq", "exp"), None))
    return jax.shard_map(body, mesh=mesh, in_specs=in_specs, out_specs=out_specs, check_vma=False)
```

```python
import jax
import jax.numpy as jnp
from jax import lax
from jax.experimental import pallas as pl
from jax.experimental.pallas import tpu as pltpu
from jax.sharding import PartitionSpec as P

NX = 4
LANES = 128
F32 = jnp.float32
BF16 = jnp.bfloat16


def seq_sizes():
    count = lax.axis_size("seq")
    return count // NX, NX


def groups_x():
    nz, nx = seq_sizes()
    return [[z * nx + x for x in range(nx)] for z in range(nz)]


def groups_z():
    nz, nx = seq_sizes()
    return [[z * nx + x for z in range(nz)] for x in range(nx)]


def send_z(block, step):
    nz, nx = seq_sizes()
    route = [
        (z * nx + x, ((z + step) % nz) * nx + x) for z in range(nz) for x in range(nx)
    ]
    return lax.ppermute(block, "seq", route)


def send_x(block, step):
    nz, nx = seq_sizes()
    route = [(z * nx + x, z * nx + (x + step) % nx) for z in range(nz) for x in range(nx)]
    return lax.ppermute(block, "seq", route)


def padded(block, before, behind):
    return jnp.pad(block.astype(F32), ((before, behind), (0, 0)))


def sum_z(parts):
    half = parts[0].shape[0] // 2
    up = send_z(parts[4][:half], 1)
    down = send_z(parts[4][half:], -1)
    up = send_z((parts[3] + padded(up, 0, half)).astype(BF16), 1)
    down = send_z((parts[5] + padded(down, half, 0)).astype(BF16), -1)
    up = send_z((parts[2] + up.astype(F32)).astype(BF16), 1)
    down = send_z((parts[6] + down.astype(F32)).astype(BF16), -1)
    up = send_z((parts[1] + up.astype(F32)).astype(BF16), 1)
    down = send_z((parts[7] + down.astype(F32)).astype(BF16), -1)
    return parts[0] + up.astype(F32) + down.astype(F32)


def sum_x_first(parts):
    half = parts[2].shape[0] // 2
    return send_x(parts[2][:half], 1), send_x(parts[2][half:], -1)


def sum_x_second(parts, came):
    half = parts[2].shape[0] // 2
    up = send_x((parts[1] + padded(came[0], 0, half)).astype(BF16), 1)
    down = send_x((parts[3] + padded(came[1], half, 0)).astype(BF16), -1)
    return parts[0] + up.astype(F32) + down.astype(F32)


def sum_x_direct(parts):
    came = [send_x(parts[1], 1), send_x(parts[2], 2), send_x(parts[3], -1)]
    total = parts[0].astype(F32)
    for part in came:
        total = total + part.astype(F32)
    return total


def scan_kernel(
    low_ref, weight_ref, bias_ref, rates_ref, act_ref, maps_ref, out_ref, passed_ref, ends_ref,
    delta_ref, driven_ref,
):
    rows, width = act_ref.shape
    states = rates_ref.shape[0]
    tiles = width // LANES
    raw = jnp.dot(low_ref[...], weight_ref[...], preferred_element_type=F32) + bias_ref[...]
    delta = jnp.maximum(raw, 0.0) + jnp.log1p(jnp.exp(-jnp.abs(raw)))
    delta_ref[...] = delta
    driven_ref[...] = delta * act_ref[...].astype(F32)
    rate = -jnp.exp(rates_ref[...])

    def step(t, carry):
        state, passed = carry
        delta_t = delta_ref[pl.ds(t, 1), :]
        driven_t = driven_ref[pl.ds(t, 1), :]
        maps_t = maps_ref[t]
        input_t = jnp.concatenate([maps_t[:states]] * tiles, axis=1)
        output_t = jnp.concatenate([maps_t[states:]] * tiles, axis=1)
        state = jnp.exp(delta_t * rate) * state + driven_t * input_t
        passed = passed + delta_t
        out_ref[pl.ds(t, 1), :] = jnp.sum(output_t * state, axis=0, keepdims=True)
        passed_ref[pl.ds(t, 1), :] = passed
        return state, passed

    state, passed = lax.fori_loop(
        0, rows, step, (jnp.zeros((states, width), F32), jnp.zeros((1, width), F32)), unroll=4
    )
    ends_ref[:states, :] = state
    ends_ref[states:, :] = passed


def finish_kernel(
    local_ref, passed_ref, start_ref, rates_ref, maps_ref, act_ref, skip_ref, gate_ref, gated_ref,
    full_ref,
):
    rows, width = act_ref.shape
    states = rates_ref.shape[0]
    tiles = width // LANES
    rate = -jnp.exp(rates_ref[...])
    start = start_ref[...]

    def step(t, carry):
        left = jnp.exp(passed_ref[pl.ds(t, 1), :] * rate) * start
        output_t = jnp.concatenate([maps_ref[t][states:]] * tiles, axis=1)
        full_ref[pl.ds(t, 1), :] = local_ref[pl.ds(t, 1), :] + jnp.sum(
            output_t * left, axis=0, keepdims=True
        )
        return carry

    lax.fori_loop(0, rows, step, 0, unroll=4)
    gate = gate_ref[...].astype(F32)
    scan_out = full_ref[...] + skip_ref[...] * act_ref[...].astype(F32)
    gated_ref[...] = (scan_out * (gate / (1.0 + jnp.exp(-gate)))).astype(BF16)


VMEM = pl.BlockSpec(memory_space=pltpu.VMEM)


def local_scan(low, weight, bias, rates, act, maps):
    rows, width = act.shape
    return pl.pallas_call(
        scan_kernel,
        out_shape=(
            jax.ShapeDtypeStruct((rows, width), F32),
            jax.ShapeDtypeStruct((rows, width), F32),
            jax.ShapeDtypeStruct((rates.shape[0] + 1, width), F32),
        ),
        in_specs=[VMEM] * 6,
        out_specs=(VMEM,) * 3,
        scratch_shapes=[pltpu.VMEM((rows, width), F32), pltpu.VMEM((rows, width), F32)],
        compiler_params=pltpu.CompilerParams(vmem_limit_bytes=16 * 2**20),
    )(low, weight, bias, rates, act, maps)


def finish_scan(local, passed, start, rates, maps, act, skip, gate):
    rows, width = act.shape
    return pl.pallas_call(
        finish_kernel,
        out_shape=jax.ShapeDtypeStruct((rows, width), BF16),
        in_specs=[VMEM] * 8,
        out_specs=VMEM,
        scratch_shapes=[pltpu.VMEM((rows, width), F32)],
        compiler_params=pltpu.CompilerParams(vmem_limit_bytes=16 * 2**20),
    )(local, passed, start, rates, maps, act, skip, gate)


def expert_kernel(count, steps, *refs):
    rows = refs[:count]
    gate_ref, up_ref, down_ref = refs[count : count + 3]
    outs = refs[count + 3 : 2 * count + 3]
    gate_sum, up_sum, act_ref = refs[2 * count + 3 :]
    size = rows[0].shape[0]
    i = pl.program_id(0)

    @pl.when(i < steps)
    def _():
        taken = jnp.concatenate([r[...] for r in rows], axis=0)
        across = (((1,), (1,)), ((), ()))
        gate = lax.dot_general(taken, gate_ref[...], across, preferred_element_type=F32)
        up = lax.dot_general(taken, up_ref[...], across, preferred_element_type=F32)

        @pl.when(i == 0)
        def _():
            gate_sum[...] = gate
            up_sum[...] = up

        @pl.when(i > 0)
        def _():
            gate_sum[...] += gate
            up_sum[...] += up

    @pl.when(i >= steps)
    def _():
        @pl.when(i == steps)
        def _():
            gate = gate_sum[...]
            act_ref[...] = (gate / (1.0 + jnp.exp(-gate)) * up_sum[...]).astype(BF16)

        out = jnp.dot(act_ref[...], down_ref[...], preferred_element_type=F32).astype(BF16)
        for k in range(count):
            outs[k][...] = out[k * size : (k + 1) * size]


def experts_of(blocks, gate_local, up_local, down_local):
    count = len(blocks)
    size, features = blocks[0].shape
    hidden = gate_local.shape[0]
    steps = 2
    width = features // steps
    early = lambda i: jnp.minimum(i, steps - 1)
    late = lambda i: jnp.maximum(i - steps, 0)
    flops = 6 * count * size * features * hidden
    moved = 6 * features * hidden + 4 * count * size * features
    return pl.pallas_call(
        lambda *refs: expert_kernel(count, steps, *refs),
        grid=(2 * steps,),
        out_shape=[jax.ShapeDtypeStruct((size, features), BF16)] * count,
        in_specs=[pl.BlockSpec((size, width), lambda i: (0, early(i)))] * count
        + [pl.BlockSpec((hidden, width), lambda i: (0, early(i)))] * 2
        + [pl.BlockSpec((hidden, width), lambda i: (0, late(i)))],
        out_specs=[pl.BlockSpec((size, width), lambda i: (0, late(i)))] * count,
        scratch_shapes=[
            pltpu.VMEM((count * size, hidden), F32),
            pltpu.VMEM((count * size, hidden), F32),
            pltpu.VMEM((count * size, hidden), BF16),
        ],
        cost_estimate=pl.CostEstimate(
            flops=flops, bytes_accessed=moved, transcendentals=count * size * hidden
        ),
        compiler_params=pltpu.CompilerParams(vmem_limit_bytes=36 * 2**20),
    )(*blocks, gate_local, up_local, down_local)


def exchanged(blocks, group):
    return lax.all_to_all(
        blocks, "seq", split_axis=0, concat_axis=0, tiled=True, axis_index_groups=group
    )


def after(ends, took, state, rate):
    return jnp.exp(-took * rate) * state + ends


def entering(ends, log_rates):
    nz, nx = seq_sizes()
    states, width = log_rates.shape
    share = width // nx
    z, x = lax.axis_index("seq") // nx, lax.axis_index("seq") % nx
    rate = jnp.exp(lax.dynamic_slice_in_dim(log_rates, x * share, share, axis=1))
    shares = ends.reshape(states + 1, nx, share).transpose(1, 0, 2)
    row = exchanged(shares, groups_x())
    state, took = jnp.zeros(rate.shape, F32), jnp.zeros((1, share), F32)
    for k in range(nx):
        state = after(row[k, :states], row[k, states:], state, rate)
        took = took + row[k, states:]
    total = jnp.concatenate([state, took])
    rows = exchanged(jnp.broadcast_to(total[None], (nz, *total.shape)), groups_z())
    state = jnp.zeros(rate.shape, F32)
    for k in range(nz - 1):
        state = jnp.where(k < z, after(rows[k, :states], rows[k, states:], state, rate), state)
    starts = [state]
    for k in range(nx - 1):
        starts.append(after(row[k, :states], row[k, states:], starts[-1], rate))
    return exchanged(jnp.stack(starts), groups_x()).transpose(1, 0, 2).reshape(states, width)


def mixer(
    mixer_input, gate_input, conv_weight, conv_bias, rank_weight, state_weight, delta_weight,
    delta_bias, log_rates, skip_gain, out_proj,
):
    taps = conv_weight.shape[0]
    block_rows = mixer_input.shape[0]
    nz, nx = seq_sizes()
    experts = lax.axis_size("exp")
    columns = lax.all_gather(
        out_proj, "seq", axis=1, tiled=True, axis_index_groups=groups_z()
    )
    rim_rows = lax.ppermute(
        mixer_input[block_rows - (taps - 1) :], "seq", [(i, i + 1) for i in range(nz * nx - 1)]
    )
    before = jnp.concatenate([rim_rows, mixer_input], axis=0)
    conv_sum = jnp.zeros(mixer_input.shape, F32) + conv_bias[None, :]
    for offset in range(taps):
        conv_sum = conv_sum + conv_weight[offset].astype(F32)[None, :] * before[
            offset : offset + block_rows
        ].astype(F32)
    conv_act = jax.nn.silu(conv_sum).astype(BF16)
    both = jnp.concatenate([rank_weight, state_weight], axis=1)
    sums = jnp.dot(conv_act, both, preferred_element_type=F32)
    rank = rank_weight.shape[1]
    coarse = lax.reduce_precision(sums, 8, 7)
    fine = sums[:, rank:] - coarse[:, rank:]
    sent = jnp.concatenate([coarse, fine], axis=1).astype(BF16)
    summed = jnp.sum(lax.all_gather(sent, "exp").astype(F32), axis=0)
    maps = summed[:, rank : sums.shape[1]] + summed[:, sums.shape[1] :]
    delta_low = summed[:, :rank].astype(BF16)
    wide_maps = jnp.broadcast_to(maps[:, :, None], (*maps.shape, LANES))
    local, passed, ends = local_scan(
        delta_low, delta_weight, delta_bias[None], log_rates, conv_act, wide_maps
    )
    start = entering(ends, log_rates)
    gated = finish_scan(
        local, passed, start, log_rates, wide_maps, conv_act, skip_gain[None], gate_input
    )
    gated_row = lax.all_gather(gated, "seq", axis=0, tiled=True, axis_index_groups=groups_x())
    partial_value = jnp.dot(gated_row, columns, preferred_element_type=F32).astype(BF16)
    planes = [
        [(k * nx + i) * experts + e for i in range(nx) for e in range(experts)] for k in range(nz)
    ]
    came = lax.all_to_all(
        partial_value, ("seq", "exp"), split_axis=0, concat_axis=0, tiled=True,
        axis_index_groups=planes,
    )
    own_rows = block_rows // experts
    came = came.reshape(nx, experts, own_rows, nz, -1).astype(F32)
    return jnp.sum(came, axis=1).transpose(1, 2, 0, 3).reshape(own_rows, -1)


def body(
    mixer_input,
    gate_input,
    conv_weight,
    conv_bias,
    rank_weight,
    state_weight,
    delta_weight,
    delta_bias,
    log_rates,
    skip_gain,
    out_proj,
    residual,
    norm_gain,
    router,
    w_gate,
    w_up,
    w_down,
    routes,
):
    mamba_out = mixer(
        mixer_input, gate_input, conv_weight, conv_bias, rank_weight, state_weight,
        delta_weight, delta_bias, log_rates, skip_gain, out_proj,
    )
    tok_dev = residual.shape[0]
    hidden = residual.astype(F32) + mamba_out
    mean_square = jnp.mean(hidden * hidden, axis=1, keepdims=True)
    normed = (hidden * lax.rsqrt(mean_square + 1e-05) * norm_gain[None, :]).astype(BF16)
    logits = jnp.dot(normed.astype(F32), router, precision=lax.Precision.HIGHEST)
    experts = router.shape[1]
    expert_ids = jnp.arange(experts, dtype=jnp.int32)
    matches = (routes[:, :, None] == expert_ids[None, None, :]).astype(F32)
    chosen = jnp.sum(matches * logits[:, None, :], axis=2)
    route_weights = jax.nn.sigmoid(chosen - chosen[:, ::-1])
    capacity = max(2, 4 * tok_dev // experts)
    flat_ids = routes.reshape(-1)
    route_pos = jnp.arange(flat_ids.shape[0], dtype=jnp.int32)
    earlier_same = (flat_ids[:, None] == flat_ids[None, :]) & (
        route_pos[None, :] < route_pos[:, None]
    )
    slot_rank = jnp.sum(earlier_same.astype(jnp.int32), axis=1)
    slot_of = (flat_ids * capacity + slot_rank).reshape(tok_dev, 2)
    slot_ids = jnp.arange(experts * capacity, dtype=jnp.int32)
    taken = slot_of[:, :, None] == slot_ids[None, None, :]
    placing = jnp.sum(taken.astype(F32), axis=1).astype(BF16)
    outbound = lax.dot_general(
        placing, normed, (((0,), (0,)), ((), ())), preferred_element_type=F32
    ).astype(BF16)
    arrived = lax.all_to_all(outbound, "exp", split_axis=0, concat_axis=0, tiled=True)
    gate_local, up_local, down_local = w_gate[0].T, w_up[0].T, w_down[0]

    def expert_list(blocks):
        return experts_of(blocks, gate_local, up_local, down_local)

    half = arrived.shape[0] // 2
    first, second = arrived[:half], arrived[half:]
    after = lax.optimization_barrier
    line_b1, line_a1 = send_z(second, 1), send_z(second, -1)
    quad = [first, send_x(first, -1), send_x(first, 2), send_x(first, 1)]
    line_b2, line_a2 = send_z(line_b1, 1), send_z(line_a1, -1)
    quad, line_b2, line_a2 = after((jnp.concatenate(quad), line_b2, line_a2))
    near_0 = jnp.concatenate([second, line_a1, line_b1, line_a2])
    near_a1, near_b1 = send_x(near_0, -1), send_x(near_0, 1)
    line_b3, line_a3 = send_z(line_b2, 1), send_z(line_a2, -1)
    quad_b1, quad_a1 = send_z(quad, 1), send_z(quad, -1)
    line_4 = [send_z(line_b3[: half // 2], 1), send_z(line_a3[half // 2 :], -1)]
    cut = near_0.shape[0] // 2
    near_2 = jnp.concatenate([send_x(near_b1[:cut], 1), send_x(near_a1[cut:], -1)])
    far_0 = jnp.concatenate([line_b2, line_a3, line_b3, *line_4])
    far_0, near_b1, near_a1 = after((far_0, near_b1, near_a1))
    far_a1, far_b1 = send_x(far_0, -1), send_x(far_0, 1)
    far_2 = jnp.concatenate([send_x(far_b1[:cut], 1), send_x(far_a1[cut:], -1)])
    quad_b2, quad_a2 = send_z(quad_b1, 1), send_z(quad_a1, -1)
    near_2, quad_b1, quad_a1 = after((near_2, quad_b1, quad_a1))
    near_out = expert_list([near_0, near_a1, near_2, near_b1])
    quad_b3, quad_a3 = send_z(quad_b2, 1), send_z(quad_a2, -1)
    far_2, quad_b2, quad_a2 = after((far_2, quad_b2, quad_a2))
    quad_out = dict(
        zip((0, 1, 7, 2, 6), expert_list([quad, quad_a1, quad_b1, quad_a2, quad_b2]))
    )
    far_out = expert_list([far_0, far_a1, far_2, far_b1])
    cut_quad = quad.shape[0] // 2
    quad_4 = jnp.concatenate([send_z(quad_b3[:cut_quad], 1), send_z(quad_a3[cut_quad:], -1)])
    far_out, quad_b3, quad_a3 = after((far_out, quad_b3, quad_a3))
    far_came = sum_x_first(far_out)
    quad_out.update(zip((3, 5, 4), expert_list([quad_a3, quad_b3, quad_4])))
    far_sum = sum_x_second(far_out, far_came)
    near_out, far_came = after((near_out, far_came))
    near_sum = sum_x_second(near_out, sum_x_first(near_out))
    quad_sum = sum_z([quad_out[d] for d in range(8)]).astype(BF16)
    first_sum = sum_x_direct([quad_sum[k * half : (k + 1) * half] for k in range(NX)])
    line_sum = {}
    for order, total in (((0, 1, 7, 2), near_sum), ((6, 3, 5, 4), far_sum)):
        for k, d in enumerate(order):
            line_sum[d] = total[k * half : (k + 1) * half].astype(BF16)
    second_sum = sum_z([line_sum[d] for d in range(8)])

    expert_out = jnp.concatenate([first_sum, second_sum]).astype(BF16)
    returned = lax.all_to_all(expert_out, "exp", split_axis=0, concat_axis=0, tiled=True)
    mixing = jnp.sum(taken.astype(F32) * route_weights[:, :, None], axis=1)
    moe_sum = jnp.dot(mixing, returned.astype(F32), precision=lax.Precision.HIGHEST)
    return ((hidden + moe_sum).astype(BF16), moe_sum)


def solution(mesh):
    in_specs = (
        P("seq", "exp"),
        P("seq", "exp"),
        P(None, "exp"),
        P("exp"),
        P("exp", None),
        P("exp", None),
        P(None, "exp"),
        P("exp"),
        P(None, "exp"),
        P("exp"),
        P("exp", "seq"),
        P(("seq", "exp"), None),
        P(),
        P(),
        P("exp", None, "seq"),
        P("exp", None, "seq"),
        P("exp", "seq", None),
        P(("seq", "exp"), None),
    )
    out_specs = (P(("seq", "exp"), None), P(("seq", "exp"), None))
    return jax.shard_map(body, mesh=mesh, in_specs=in_specs, out_specs=out_specs, check_vma=False)
```

```python
import jax
import jax.numpy as jnp
from jax import lax
from jax.experimental import pallas as pl
from jax.experimental.pallas import tpu as pltpu
from jax.sharding import PartitionSpec as P

NX = 4
LANES = 128
F32 = jnp.float32
BF16 = jnp.bfloat16


def seq_sizes():
    count = lax.axis_size("seq")
    return count // NX, NX


def groups_x():
    nz, nx = seq_sizes()
    return [[z * nx + x for x in range(nx)] for z in range(nz)]


def groups_z():
    nz, nx = seq_sizes()
    return [[z * nx + x for z in range(nz)] for x in range(nx)]


def send_z(block, step):
    nz, nx = seq_sizes()
    route = [
        (z * nx + x, ((z + step) % nz) * nx + x) for z in range(nz) for x in range(nx)
    ]
    return lax.ppermute(block, "seq", route)


def send_x(block, step):
    nz, nx = seq_sizes()
    route = [(z * nx + x, z * nx + (x + step) % nx) for z in range(nz) for x in range(nx)]
    return lax.ppermute(block, "seq", route)


def padded(block, before, behind):
    return jnp.pad(block.astype(F32), ((before, behind), (0, 0)))


def sum_z_steps(parts):
    half = parts[4].shape[0] // 2
    came = yield send_z(parts[4][:half], 1), send_z(parts[4][half:], -1)
    rest = parts[4].shape[0] - half
    came = yield (
        send_z((parts[3] + padded(came[0], 0, rest)).astype(BF16), 1),
        send_z((parts[5] + padded(came[1], half, 0)).astype(BF16), -1),
    )
    for up, down in ((2, 6), (1, 7)):
        came = yield (
            send_z((parts[up] + came[0].astype(F32)).astype(BF16), 1),
            send_z((parts[down] + came[1].astype(F32)).astype(BF16), -1),
        )
    yield parts[0] + came[0].astype(F32) + came[1].astype(F32)


def sum_x_first(parts):
    half = parts[2].shape[0] // 2
    return send_x(parts[2][:half], 1), send_x(parts[2][half:], -1)


def sum_x_second(parts, came):
    half = parts[2].shape[0] // 2
    up = send_x((parts[1] + padded(came[0], 0, half)).astype(BF16), 1)
    down = send_x((parts[3] + padded(came[1], half, 0)).astype(BF16), -1)
    return parts[0] + up.astype(F32) + down.astype(F32)


def sum_x_direct(parts):
    came = [send_x(parts[1], 1), send_x(parts[2], 2), send_x(parts[3], -1)]
    total = parts[0].astype(F32)
    for part in came:
        total = total + part.astype(F32)
    return total


def scan_kernel(
    low_ref, weight_ref, bias_ref, rates_ref, act_ref, maps_ref, out_ref, passed_ref, ends_ref,
    delta_ref, driven_ref,
):
    rows, width = act_ref.shape
    states = rates_ref.shape[0]
    tiles = width // LANES
    raw = jnp.dot(low_ref[...], weight_ref[...], preferred_element_type=F32) + bias_ref[...]
    delta = jnp.maximum(raw, 0.0) + jnp.log1p(jnp.exp(-jnp.abs(raw)))
    delta_ref[...] = delta
    driven_ref[...] = delta * act_ref[...].astype(F32)
    rate = -jnp.exp(rates_ref[...])

    def step(t, carry):
        state, passed = carry
        delta_t = delta_ref[pl.ds(t, 1), :]
        driven_t = driven_ref[pl.ds(t, 1), :]
        maps_t = maps_ref[t]
        input_t = jnp.concatenate([maps_t[:states]] * tiles, axis=1)
        output_t = jnp.concatenate([maps_t[states:]] * tiles, axis=1)
        state = jnp.exp(delta_t * rate) * state + driven_t * input_t
        passed = passed + delta_t
        out_ref[pl.ds(t, 1), :] = jnp.sum(output_t * state, axis=0, keepdims=True)
        passed_ref[pl.ds(t, 1), :] = passed
        return state, passed

    state, passed = lax.fori_loop(
        0, rows, step, (jnp.zeros((states, width), F32), jnp.zeros((1, width), F32)), unroll=4
    )
    ends_ref[:states, :] = state
    ends_ref[states:, :] = passed


def finish_kernel(
    local_ref, passed_ref, start_ref, rates_ref, maps_ref, act_ref, skip_ref, gate_ref, gated_ref,
    full_ref,
):
    rows, width = act_ref.shape
    states = rates_ref.shape[0]
    tiles = width // LANES
    rate = -jnp.exp(rates_ref[...])
    start = start_ref[...]

    def step(t, carry):
        left = jnp.exp(passed_ref[pl.ds(t, 1), :] * rate) * start
        output_t = jnp.concatenate([maps_ref[t][states:]] * tiles, axis=1)
        full_ref[pl.ds(t, 1), :] = local_ref[pl.ds(t, 1), :] + jnp.sum(
            output_t * left, axis=0, keepdims=True
        )
        return carry

    lax.fori_loop(0, rows, step, 0, unroll=4)
    gate = gate_ref[...].astype(F32)
    scan_out = full_ref[...] + skip_ref[...] * act_ref[...].astype(F32)
    gated_ref[...] = (scan_out * (gate / (1.0 + jnp.exp(-gate)))).astype(BF16)


VMEM = pl.BlockSpec(memory_space=pltpu.VMEM)


def local_scan(low, weight, bias, rates, act, maps):
    rows, width = act.shape
    return pl.pallas_call(
        scan_kernel,
        out_shape=(
            jax.ShapeDtypeStruct((rows, width), F32),
            jax.ShapeDtypeStruct((rows, width), F32),
            jax.ShapeDtypeStruct((rates.shape[0] + 1, width), F32),
        ),
        in_specs=[VMEM] * 6,
        out_specs=(VMEM,) * 3,
        scratch_shapes=[pltpu.VMEM((rows, width), F32), pltpu.VMEM((rows, width), F32)],
        compiler_params=pltpu.CompilerParams(vmem_limit_bytes=16 * 2**20),
    )(low, weight, bias, rates, act, maps)


def finish_scan(local, passed, start, rates, maps, act, skip, gate):
    rows, width = act.shape
    return pl.pallas_call(
        finish_kernel,
        out_shape=jax.ShapeDtypeStruct((rows, width), BF16),
        in_specs=[VMEM] * 8,
        out_specs=VMEM,
        scratch_shapes=[pltpu.VMEM((rows, width), F32)],
        compiler_params=pltpu.CompilerParams(vmem_limit_bytes=16 * 2**20),
    )(local, passed, start, rates, maps, act, skip, gate)


def expert_kernel(count, steps, *refs):
    rows = refs[:count]
    gate_ref, up_ref, down_ref = refs[count : count + 3]
    outs = refs[count + 3 : 2 * count + 3]
    gate_sum, up_sum, act_ref = refs[2 * count + 3 :]
    size = rows[0].shape[0]
    i = pl.program_id(0)

    @pl.when(i < steps)
    def _():
        taken = jnp.concatenate([r[...] for r in rows], axis=0)
        across = (((1,), (1,)), ((), ()))
        gate = lax.dot_general(taken, gate_ref[...], across, preferred_element_type=F32)
        up = lax.dot_general(taken, up_ref[...], across, preferred_element_type=F32)

        @pl.when(i == 0)
        def _():
            gate_sum[...] = gate
            up_sum[...] = up

        @pl.when(i > 0)
        def _():
            gate_sum[...] += gate
            up_sum[...] += up

    @pl.when(i >= steps)
    def _():
        @pl.when(i == steps)
        def _():
            gate = gate_sum[...]
            act_ref[...] = (gate / (1.0 + jnp.exp(-gate)) * up_sum[...]).astype(BF16)

        out = jnp.dot(act_ref[...], down_ref[...], preferred_element_type=F32).astype(BF16)
        for k in range(count):
            outs[k][...] = out[k * size : (k + 1) * size]


def experts_of(blocks, gate_local, up_local, down_local):
    count = len(blocks)
    size, features = blocks[0].shape
    hidden = gate_local.shape[0]
    steps = 2
    width = features // steps
    early = lambda i: jnp.minimum(i, steps - 1)
    late = lambda i: jnp.maximum(i - steps, 0)
    flops = 6 * count * size * features * hidden
    moved = 6 * features * hidden + 4 * count * size * features
    return pl.pallas_call(
        lambda *refs: expert_kernel(count, steps, *refs),
        grid=(2 * steps,),
        out_shape=[jax.ShapeDtypeStruct((size, features), BF16)] * count,
        in_specs=[pl.BlockSpec((size, width), lambda i: (0, early(i)))] * count
        + [pl.BlockSpec((hidden, width), lambda i: (0, early(i)))] * 2
        + [pl.BlockSpec((hidden, width), lambda i: (0, late(i)))],
        out_specs=[pl.BlockSpec((size, width), lambda i: (0, late(i)))] * count,
        scratch_shapes=[
            pltpu.VMEM((count * size, hidden), F32),
            pltpu.VMEM((count * size, hidden), F32),
            pltpu.VMEM((count * size, hidden), BF16),
        ],
        cost_estimate=pl.CostEstimate(
            flops=flops, bytes_accessed=moved, transcendentals=count * size * hidden
        ),
        compiler_params=pltpu.CompilerParams(vmem_limit_bytes=36 * 2**20),
    )(*blocks, gate_local, up_local, down_local)


def exchanged(blocks, group):
    return lax.all_to_all(
        blocks, "seq", split_axis=0, concat_axis=0, tiled=True, axis_index_groups=group
    )


def after(ends, took, state, rate):
    return jnp.exp(-took * rate) * state + ends


def entering(ends, log_rates):
    nz, nx = seq_sizes()
    states, width = log_rates.shape
    share = width // nx
    z, x = lax.axis_index("seq") // nx, lax.axis_index("seq") % nx
    rate = jnp.exp(lax.dynamic_slice_in_dim(log_rates, x * share, share, axis=1))
    shares = ends.reshape(states + 1, nx, share).transpose(1, 0, 2)
    row = exchanged(shares, groups_x())
    state, took = jnp.zeros(rate.shape, F32), jnp.zeros((1, share), F32)
    for k in range(nx):
        state = after(row[k, :states], row[k, states:], state, rate)
        took = took + row[k, states:]
    total = jnp.concatenate([state, took])
    rows = exchanged(jnp.broadcast_to(total[None], (nz, *total.shape)), groups_z())
    state = jnp.zeros(rate.shape, F32)
    for k in range(nz - 1):
        state = jnp.where(k < z, after(rows[k, :states], rows[k, states:], state, rate), state)
    starts = [state]
    for k in range(nx - 1):
        starts.append(after(row[k, :states], row[k, states:], starts[-1], rate))
    return exchanged(jnp.stack(starts), groups_x()).transpose(1, 0, 2).reshape(states, width)


def mixer(
    mixer_input, gate_input, conv_weight, conv_bias, rank_weight, state_weight, delta_weight,
    delta_bias, log_rates, skip_gain, out_proj,
):
    taps = conv_weight.shape[0]
    block_rows = mixer_input.shape[0]
    nz, nx = seq_sizes()
    experts = lax.axis_size("exp")
    columns = lax.all_gather(
        out_proj, "seq", axis=1, tiled=True, axis_index_groups=groups_z()
    )
    rim_rows = lax.ppermute(
        mixer_input[block_rows - (taps - 1) :], "seq", [(i, i + 1) for i in range(nz * nx - 1)]
    )
    before = jnp.concatenate([rim_rows, mixer_input], axis=0)
    conv_sum = jnp.zeros(mixer_input.shape, F32) + conv_bias[None, :]
    for offset in range(taps):
        conv_sum = conv_sum + conv_weight[offset].astype(F32)[None, :] * before[
            offset : offset + block_rows
        ].astype(F32)
    conv_act = jax.nn.silu(conv_sum).astype(BF16)
    both = jnp.concatenate([rank_weight, state_weight], axis=1)
    sums = jnp.dot(conv_act, both, preferred_element_type=F32)
    rank = rank_weight.shape[1]
    coarse = lax.reduce_precision(sums, 8, 7)
    fine = sums[:, rank:] - coarse[:, rank:]
    sent = jnp.concatenate([coarse, fine], axis=1).astype(BF16)
    summed = jnp.sum(lax.all_gather(sent, "exp").astype(F32), axis=0)
    maps = summed[:, rank : sums.shape[1]] + summed[:, sums.shape[1] :]
    delta_low = summed[:, :rank].astype(BF16)
    wide_maps = jnp.broadcast_to(maps[:, :, None], (*maps.shape, LANES))
    local, passed, ends = local_scan(
        delta_low, delta_weight, delta_bias[None], log_rates, conv_act, wide_maps
    )
    start = entering(ends, log_rates)
    gated = finish_scan(
        local, passed, start, log_rates, wide_maps, conv_act, skip_gain[None], gate_input
    )
    gated_row = lax.all_gather(gated, "seq", axis=0, tiled=True, axis_index_groups=groups_x())
    partial_value = jnp.dot(gated_row, columns, preferred_element_type=F32).astype(BF16)
    planes = [
        [(k * nx + i) * experts + e for i in range(nx) for e in range(experts)] for k in range(nz)
    ]
    came = lax.all_to_all(
        partial_value, ("seq", "exp"), split_axis=0, concat_axis=0, tiled=True,
        axis_index_groups=planes,
    )
    own_rows = block_rows // experts
    came = came.reshape(nx, experts, own_rows, nz, -1).astype(F32)
    return jnp.sum(came, axis=1).transpose(1, 2, 0, 3).reshape(own_rows, -1)


def body(
    mixer_input,
    gate_input,
    conv_weight,
    conv_bias,
    rank_weight,
    state_weight,
    delta_weight,
    delta_bias,
    log_rates,
    skip_gain,
    out_proj,
    residual,
    norm_gain,
    router,
    w_gate,
    w_up,
    w_down,
    routes,
):
    mamba_out = mixer(
        mixer_input, gate_input, conv_weight, conv_bias, rank_weight, state_weight,
        delta_weight, delta_bias, log_rates, skip_gain, out_proj,
    )
    tok_dev = residual.shape[0]
    hidden = residual.astype(F32) + mamba_out
    mean_square = jnp.mean(hidden * hidden, axis=1, keepdims=True)
    normed = (hidden * lax.rsqrt(mean_square + 1e-05) * norm_gain[None, :]).astype(BF16)
    logits = jnp.dot(normed.astype(F32), router, precision=lax.Precision.HIGHEST)
    experts = router.shape[1]
    expert_ids = jnp.arange(experts, dtype=jnp.int32)
    matches = (routes[:, :, None] == expert_ids[None, None, :]).astype(F32)
    chosen = jnp.sum(matches * logits[:, None, :], axis=2)
    route_weights = jax.nn.sigmoid(chosen - chosen[:, ::-1])
    capacity = max(2, 4 * tok_dev // experts)
    flat_ids = routes.reshape(-1)
    route_pos = jnp.arange(flat_ids.shape[0], dtype=jnp.int32)
    earlier_same = (flat_ids[:, None] == flat_ids[None, :]) & (
        route_pos[None, :] < route_pos[:, None]
    )
    slot_rank = jnp.sum(earlier_same.astype(jnp.int32), axis=1)
    slot_of = (flat_ids * capacity + slot_rank).reshape(tok_dev, 2)
    slot_ids = jnp.arange(experts * capacity, dtype=jnp.int32)
    taken = slot_of[:, :, None] == slot_ids[None, None, :]
    placing = jnp.sum(taken.astype(F32), axis=1).astype(BF16)
    outbound = lax.dot_general(
        placing, normed, (((0,), (0,)), ((), ())), preferred_element_type=F32
    ).astype(BF16)
    arrived = lax.all_to_all(outbound, "exp", split_axis=0, concat_axis=0, tiled=True)
    gate_local, up_local, down_local = w_gate[0].T, w_up[0].T, w_down[0]

    def expert_list(blocks):
        return experts_of(blocks, gate_local, up_local, down_local)

    cut_rows = 3 * arrived.shape[0] // 8
    first, second = arrived[:cut_rows], arrived[cut_rows:]
    half, size = second.shape[0] // 2, second.shape[0]
    after = lax.optimization_barrier
    line_b1, line_a1 = send_z(second, 1), send_z(second, -1)
    quad = [first, send_x(first, -1), send_x(first, 2), send_x(first, 1)]
    line_b2, line_a2 = send_z(line_b1, 1), send_z(line_a1, -1)
    quad, line_b2, line_a2 = after((jnp.concatenate(quad), line_b2, line_a2))
    near_0 = jnp.concatenate([second, line_a1, line_b1, line_a2])
    near_a1, near_b1 = send_x(near_0, -1), send_x(near_0, 1)
    line_b3, line_a3 = send_z(line_b2, 1), send_z(line_a2, -1)
    quad_b1, quad_a1 = send_z(quad, 1), send_z(quad, -1)
    line_4 = [send_z(line_b3[:half], 1), send_z(line_a3[half:], -1)]
    cut = near_0.shape[0] // 2
    near_2 = jnp.concatenate([send_x(near_b1[:cut], 1), send_x(near_a1[cut:], -1)])
    far_0 = jnp.concatenate([line_b2, line_a3, line_b3, *line_4])
    far_0, near_b1, near_a1 = after((far_0, near_b1, near_a1))
    far_a1, far_b1 = send_x(far_0, -1), send_x(far_0, 1)
    far_2 = jnp.concatenate([send_x(far_b1[:cut], 1), send_x(far_a1[cut:], -1)])
    quad_b2, quad_a2 = send_z(quad_b1, 1), send_z(quad_a1, -1)
    near_2, quad_b1, quad_a1 = after((near_2, quad_b1, quad_a1))
    near_out = expert_list([near_0, near_a1, near_2, near_b1])
    quad_b3, quad_a3 = send_z(quad_b2, 1), send_z(quad_a2, -1)
    far_2, quad_b2, quad_a2 = after((far_2, quad_b2, quad_a2))
    far_out = expert_list([far_0, far_a1, far_2, far_b1])
    cut_quad = quad.shape[0] // 2
    quad_4 = jnp.concatenate([send_z(quad_b3[:cut_quad], 1), send_z(quad_a3[cut_quad:], -1)])
    far_out, quad_a2, quad_b3, quad_a3 = after((far_out, quad_a2, quad_b3, quad_a3))
    quad_out = dict(
        zip((0, 1, 7, 2, 6), expert_list([quad, quad_a1, quad_b1, quad_a2, quad_b2]))
    )
    far_came = sum_x_first(far_out)
    quad_out.update(zip((3, 5, 4), expert_list([quad_a3, quad_b3, quad_4])))
    far_sum = sum_x_second(far_out, far_came)
    near_out, far_came = after((near_out, far_came))
    near_sum = sum_x_second(near_out, sum_x_first(near_out))
    line_sum = {}
    for order, total in (((0, 1, 7, 2), near_sum), ((6, 3, 5, 4), far_sum)):
        for k, d in enumerate(order):
            line_sum[d] = total[k * size : (k + 1) * size].astype(BF16)
    quad_steps, line_steps = sum_z_steps(quad_out), sum_z_steps(line_sum)
    quad_came, line_came = next(quad_steps), next(line_steps)
    quad_came = quad_steps.send(quad_came)
    for _ in range(2):
        line_came = after((line_came, quad_came))[0]
        quad_came, line_came = quad_steps.send(quad_came), line_steps.send(line_came)
    quad_sum = quad_steps.send(quad_came).astype(BF16)
    line_came = line_steps.send(line_came)
    first_sum = sum_x_direct([quad_sum[k * cut_rows : (k + 1) * cut_rows] for k in range(NX)])
    second_sum = line_steps.send(line_came)

    expert_out = jnp.concatenate([first_sum, second_sum]).astype(BF16)
    returned = lax.all_to_all(expert_out, "exp", split_axis=0, concat_axis=0, tiled=True)
    mixing = jnp.sum(taken.astype(F32) * route_weights[:, :, None], axis=1)
    moe_sum = jnp.dot(mixing, returned.astype(F32), precision=lax.Precision.HIGHEST)
    return ((hidden + moe_sum).astype(BF16), moe_sum)


def solution(mesh):
    in_specs = (
        P("seq", "exp"),
        P("seq", "exp"),
        P(None, "exp"),
        P("exp"),
        P("exp", None),
        P("exp", None),
        P(None, "exp"),
        P("exp"),
        P(None, "exp"),
        P("exp"),
        P("exp", "seq"),
        P(("seq", "exp"), None),
        P(),
        P(),
        P("exp", None, "seq"),
        P("exp", None, "seq"),
        P("exp", "seq", None),
        P(("seq", "exp"), None),
    )
    out_specs = (P(("seq", "exp"), None), P(("seq", "exp"), None))
    return jax.shard_map(body, mesh=mesh, in_specs=in_specs, out_specs=out_specs, check_vma=False)
```

```python
import jax
import jax.numpy as jnp
from jax import lax
from jax.experimental import pallas as pl
from jax.experimental.pallas import tpu as pltpu
from jax.sharding import PartitionSpec as P

NX = 4
LANES = 128
F32 = jnp.float32
BF16 = jnp.bfloat16


def seq_sizes():
    count = lax.axis_size("seq")
    return count // NX, NX


def groups_x():
    nz, nx = seq_sizes()
    return [[z * nx + x for x in range(nx)] for z in range(nz)]


def groups_z():
    nz, nx = seq_sizes()
    return [[z * nx + x for z in range(nz)] for x in range(nx)]


def send_z(block, step):
    nz, nx = seq_sizes()
    route = [
        (z * nx + x, ((z + step) % nz) * nx + x) for z in range(nz) for x in range(nx)
    ]
    return lax.ppermute(block, "seq", route)


def send_x(block, step):
    nz, nx = seq_sizes()
    route = [(z * nx + x, z * nx + (x + step) % nx) for z in range(nz) for x in range(nx)]
    return lax.ppermute(block, "seq", route)


def padded(block, before, behind):
    return jnp.pad(block.astype(F32), ((before, behind), (0, 0)))


def sum_z_steps(parts, both):
    half = parts[4].shape[0] // 2
    if both:
        came = yield send_z(parts[4][:half], 1), send_z(parts[4][half:], -1)
        came = yield (
            send_z((parts[3] + padded(came[0], 0, half)).astype(BF16), 1),
            send_z((parts[5] + padded(came[1], half, 0)).astype(BF16), -1),
        )
    else:
        came = yield (send_z(parts[4], 1),)
        came, below = lax.optimization_barrier((came, parts[5]))
        came = yield (
            send_z((parts[3] + came[0].astype(F32)).astype(BF16), 1),
            send_z(below, -1),
        )
    for up, down in ((2, 6), (1, 7)):
        came = yield (
            send_z((parts[up] + came[0].astype(F32)).astype(BF16), 1),
            send_z((parts[down] + came[1].astype(F32)).astype(BF16), -1),
        )
    yield parts[0] + came[0].astype(F32) + came[1].astype(F32)


def sum_x_first(parts):
    half = parts[2].shape[0] // 2
    return send_x(parts[2][:half], 1), send_x(parts[2][half:], -1)


def sum_x_second(parts, came):
    half = parts[2].shape[0] // 2
    up = send_x((parts[1] + padded(came[0], 0, half)).astype(BF16), 1)
    down = send_x((parts[3] + padded(came[1], half, 0)).astype(BF16), -1)
    return parts[0] + up.astype(F32) + down.astype(F32)


def sum_x_direct(parts):
    came = [send_x(parts[1], 1), send_x(parts[2], 2), send_x(parts[3], -1)]
    total = parts[0].astype(F32)
    for part in came:
        total = total + part.astype(F32)
    return total


def scan_kernel(
    low_ref, weight_ref, bias_ref, rates_ref, act_ref, maps_ref, out_ref, passed_ref, ends_ref,
    delta_ref, driven_ref,
):
    rows, width = act_ref.shape
    states = rates_ref.shape[0]
    tiles = width // LANES
    raw = jnp.dot(low_ref[...], weight_ref[...], preferred_element_type=F32) + bias_ref[...]
    delta = jnp.maximum(raw, 0.0) + jnp.log1p(jnp.exp(-jnp.abs(raw)))
    delta_ref[...] = delta
    driven_ref[...] = delta * act_ref[...].astype(F32)
    rate = -jnp.exp(rates_ref[...])

    def step(t, carry):
        state, passed = carry
        delta_t = delta_ref[pl.ds(t, 1), :]
        driven_t = driven_ref[pl.ds(t, 1), :]
        maps_t = maps_ref[t]
        input_t = jnp.concatenate([maps_t[:states]] * tiles, axis=1)
        output_t = jnp.concatenate([maps_t[states:]] * tiles, axis=1)
        state = jnp.exp(delta_t * rate) * state + driven_t * input_t
        passed = passed + delta_t
        out_ref[pl.ds(t, 1), :] = jnp.sum(output_t * state, axis=0, keepdims=True)
        passed_ref[pl.ds(t, 1), :] = passed
        return state, passed

    state, passed = lax.fori_loop(
        0, rows, step, (jnp.zeros((states, width), F32), jnp.zeros((1, width), F32)), unroll=4
    )
    ends_ref[:states, :] = state
    ends_ref[states:, :] = passed


def finish_kernel(
    local_ref, passed_ref, start_ref, rates_ref, maps_ref, act_ref, skip_ref, gate_ref, gated_ref,
    full_ref,
):
    rows, width = act_ref.shape
    states = rates_ref.shape[0]
    tiles = width // LANES
    rate = -jnp.exp(rates_ref[...])
    start = start_ref[...]

    def step(t, carry):
        left = jnp.exp(passed_ref[pl.ds(t, 1), :] * rate) * start
        output_t = jnp.concatenate([maps_ref[t][states:]] * tiles, axis=1)
        full_ref[pl.ds(t, 1), :] = local_ref[pl.ds(t, 1), :] + jnp.sum(
            output_t * left, axis=0, keepdims=True
        )
        return carry

    lax.fori_loop(0, rows, step, 0, unroll=4)
    gate = gate_ref[...].astype(F32)
    scan_out = full_ref[...] + skip_ref[...] * act_ref[...].astype(F32)
    gated_ref[...] = (scan_out * (gate / (1.0 + jnp.exp(-gate)))).astype(BF16)


VMEM = pl.BlockSpec(memory_space=pltpu.VMEM)


def local_scan(low, weight, bias, rates, act, maps):
    rows, width = act.shape
    return pl.pallas_call(
        scan_kernel,
        out_shape=(
            jax.ShapeDtypeStruct((rows, width), F32),
            jax.ShapeDtypeStruct((rows, width), F32),
            jax.ShapeDtypeStruct((rates.shape[0] + 1, width), F32),
        ),
        in_specs=[VMEM] * 6,
        out_specs=(VMEM,) * 3,
        scratch_shapes=[pltpu.VMEM((rows, width), F32), pltpu.VMEM((rows, width), F32)],
        compiler_params=pltpu.CompilerParams(vmem_limit_bytes=16 * 2**20),
    )(low, weight, bias, rates, act, maps)


def finish_scan(local, passed, start, rates, maps, act, skip, gate):
    rows, width = act.shape
    return pl.pallas_call(
        finish_kernel,
        out_shape=jax.ShapeDtypeStruct((rows, width), BF16),
        in_specs=[VMEM] * 8,
        out_specs=VMEM,
        scratch_shapes=[pltpu.VMEM((rows, width), F32)],
        compiler_params=pltpu.CompilerParams(vmem_limit_bytes=16 * 2**20),
    )(local, passed, start, rates, maps, act, skip, gate)


def expert_kernel(count, steps, *refs):
    rows = refs[:count]
    gate_ref, up_ref, down_ref = refs[count : count + 3]
    outs = refs[count + 3 : 2 * count + 3]
    gate_sum, up_sum, act_ref = refs[2 * count + 3 :]
    size = rows[0].shape[0]
    i = pl.program_id(0)

    @pl.when(i < steps)
    def _():
        taken = jnp.concatenate([r[...] for r in rows], axis=0)
        across = (((1,), (1,)), ((), ()))
        gate = lax.dot_general(taken, gate_ref[...], across, preferred_element_type=F32)
        up = lax.dot_general(taken, up_ref[...], across, preferred_element_type=F32)

        @pl.when(i == 0)
        def _():
            gate_sum[...] = gate
            up_sum[...] = up

        @pl.when(i > 0)
        def _():
            gate_sum[...] += gate
            up_sum[...] += up

    @pl.when(i >= steps)
    def _():
        @pl.when(i == steps)
        def _():
            gate = gate_sum[...]
            act_ref[...] = (gate / (1.0 + jnp.exp(-gate)) * up_sum[...]).astype(BF16)

        out = jnp.dot(act_ref[...], down_ref[...], preferred_element_type=F32).astype(BF16)
        for k in range(count):
            outs[k][...] = out[k * size : (k + 1) * size]


def experts_of(blocks, gate_local, up_local, down_local):
    count = len(blocks)
    size, features = blocks[0].shape
    hidden = gate_local.shape[0]
    steps = 2
    width = features // steps
    early = lambda i: jnp.minimum(i, steps - 1)
    late = lambda i: jnp.maximum(i - steps, 0)
    flops = 6 * count * size * features * hidden
    moved = 6 * features * hidden + 4 * count * size * features
    return pl.pallas_call(
        lambda *refs: expert_kernel(count, steps, *refs),
        grid=(2 * steps,),
        out_shape=[jax.ShapeDtypeStruct((size, features), BF16)] * count,
        in_specs=[pl.BlockSpec((size, width), lambda i: (0, early(i)))] * count
        + [pl.BlockSpec((hidden, width), lambda i: (0, early(i)))] * 2
        + [pl.BlockSpec((hidden, width), lambda i: (0, late(i)))],
        out_specs=[pl.BlockSpec((size, width), lambda i: (0, late(i)))] * count,
        scratch_shapes=[
            pltpu.VMEM((count * size, hidden), F32),
            pltpu.VMEM((count * size, hidden), F32),
            pltpu.VMEM((count * size, hidden), BF16),
        ],
        cost_estimate=pl.CostEstimate(
            flops=flops, bytes_accessed=moved, transcendentals=count * size * hidden
        ),
        compiler_params=pltpu.CompilerParams(vmem_limit_bytes=36 * 2**20),
    )(*blocks, gate_local, up_local, down_local)


def exchanged(blocks, group):
    return lax.all_to_all(
        blocks, "seq", split_axis=0, concat_axis=0, tiled=True, axis_index_groups=group
    )


def after(ends, took, state, rate):
    return jnp.exp(-took * rate) * state + ends


def entering(ends, log_rates):
    nz, nx = seq_sizes()
    states, width = log_rates.shape
    share = width // nx
    z, x = lax.axis_index("seq") // nx, lax.axis_index("seq") % nx
    rate = jnp.exp(lax.dynamic_slice_in_dim(log_rates, x * share, share, axis=1))
    shares = ends.reshape(states + 1, nx, share).transpose(1, 0, 2)
    row = exchanged(shares, groups_x())
    state, took = jnp.zeros(rate.shape, F32), jnp.zeros((1, share), F32)
    for k in range(nx):
        state = after(row[k, :states], row[k, states:], state, rate)
        took = took + row[k, states:]
    total = jnp.concatenate([state, took])
    rows = exchanged(jnp.broadcast_to(total[None], (nz, *total.shape)), groups_z())
    state = jnp.zeros(rate.shape, F32)
    for k in range(nz - 1):
        state = jnp.where(k < z, after(rows[k, :states], rows[k, states:], state, rate), state)
    starts = [state]
    for k in range(nx - 1):
        starts.append(after(row[k, :states], row[k, states:], starts[-1], rate))
    return exchanged(jnp.stack(starts), groups_x()).transpose(1, 0, 2).reshape(states, width)


def mixer(
    mixer_input, gate_input, conv_weight, conv_bias, rank_weight, state_weight, delta_weight,
    delta_bias, log_rates, skip_gain, out_proj,
):
    taps = conv_weight.shape[0]
    block_rows = mixer_input.shape[0]
    nz, nx = seq_sizes()
    experts = lax.axis_size("exp")
    columns = lax.all_gather(
        out_proj, "seq", axis=1, tiled=True, axis_index_groups=groups_z()
    )
    rim_rows = lax.ppermute(
        mixer_input[block_rows - (taps - 1) :], "seq", [(i, i + 1) for i in range(nz * nx - 1)]
    )
    before = jnp.concatenate([rim_rows, mixer_input], axis=0)
    conv_sum = jnp.zeros(mixer_input.shape, F32) + conv_bias[None, :]
    for offset in range(taps):
        conv_sum = conv_sum + conv_weight[offset].astype(F32)[None, :] * before[
            offset : offset + block_rows
        ].astype(F32)
    conv_act = jax.nn.silu(conv_sum).astype(BF16)
    both = jnp.concatenate([rank_weight, state_weight], axis=1)
    sums = jnp.dot(conv_act, both, preferred_element_type=F32)
    rank = rank_weight.shape[1]
    coarse = lax.reduce_precision(sums, 8, 7)
    fine = sums[:, rank:] - coarse[:, rank:]
    sent = jnp.concatenate([coarse, fine], axis=1).astype(BF16)
    summed = jnp.sum(lax.all_gather(sent, "exp").astype(F32), axis=0)
    maps = summed[:, rank : sums.shape[1]] + summed[:, sums.shape[1] :]
    delta_low = summed[:, :rank].astype(BF16)
    wide_maps = jnp.broadcast_to(maps[:, :, None], (*maps.shape, LANES))
    local, passed, ends = local_scan(
        delta_low, delta_weight, delta_bias[None], log_rates, conv_act, wide_maps
    )
    start = entering(ends, log_rates)
    gated = finish_scan(
        local, passed, start, log_rates, wide_maps, conv_act, skip_gain[None], gate_input
    )
    gated_row = lax.all_gather(gated, "seq", axis=0, tiled=True, axis_index_groups=groups_x())
    partial_value = jnp.dot(gated_row, columns, preferred_element_type=F32).astype(BF16)
    planes = [
        [(k * nx + i) * experts + e for i in range(nx) for e in range(experts)] for k in range(nz)
    ]
    came = lax.all_to_all(
        partial_value, ("seq", "exp"), split_axis=0, concat_axis=0, tiled=True,
        axis_index_groups=planes,
    )
    own_rows = block_rows // experts
    came = came.reshape(nx, experts, own_rows, nz, -1).astype(F32)
    return jnp.sum(came, axis=1).transpose(1, 2, 0, 3).reshape(own_rows, -1)


def body(
    mixer_input,
    gate_input,
    conv_weight,
    conv_bias,
    rank_weight,
    state_weight,
    delta_weight,
    delta_bias,
    log_rates,
    skip_gain,
    out_proj,
    residual,
    norm_gain,
    router,
    w_gate,
    w_up,
    w_down,
    routes,
):
    mamba_out = mixer(
        mixer_input, gate_input, conv_weight, conv_bias, rank_weight, state_weight,
        delta_weight, delta_bias, log_rates, skip_gain, out_proj,
    )
    tok_dev = residual.shape[0]
    hidden = residual.astype(F32) + mamba_out
    mean_square = jnp.mean(hidden * hidden, axis=1, keepdims=True)
    normed = (hidden * lax.rsqrt(mean_square + 1e-05) * norm_gain[None, :]).astype(BF16)
    logits = jnp.dot(normed.astype(F32), router, precision=lax.Precision.HIGHEST)
    experts = router.shape[1]
    expert_ids = jnp.arange(experts, dtype=jnp.int32)
    matches = (routes[:, :, None] == expert_ids[None, None, :]).astype(F32)
    chosen = jnp.sum(matches * logits[:, None, :], axis=2)
    route_weights = jax.nn.sigmoid(chosen - chosen[:, ::-1])
    capacity = max(2, 4 * tok_dev // experts)
    flat_ids = routes.reshape(-1)
    route_pos = jnp.arange(flat_ids.shape[0], dtype=jnp.int32)
    earlier_same = (flat_ids[:, None] == flat_ids[None, :]) & (
        route_pos[None, :] < route_pos[:, None]
    )
    slot_rank = jnp.sum(earlier_same.astype(jnp.int32), axis=1)
    slot_of = (flat_ids * capacity + slot_rank).reshape(tok_dev, 2)
    slot_ids = jnp.arange(experts * capacity, dtype=jnp.int32)
    taken = slot_of[:, :, None] == slot_ids[None, None, :]
    placing = jnp.sum(taken.astype(F32), axis=1).astype(BF16)
    outbound = lax.dot_general(
        placing, normed, (((0,), (0,)), ((), ())), preferred_element_type=F32
    ).astype(BF16)
    arrived = lax.all_to_all(outbound, "exp", split_axis=0, concat_axis=0, tiled=True)
    gate_local, up_local, down_local = w_gate[0].T, w_up[0].T, w_down[0]

    def expert_list(blocks):
        return experts_of(blocks, gate_local, up_local, down_local)

    cut_rows = arrived.shape[0] // 2
    first, second = arrived[:cut_rows], arrived[cut_rows:]
    size = second.shape[0]
    after = lax.optimization_barrier
    line_b1, line_a1 = send_z(second, 1), send_z(second, -1)
    quad = [first, send_x(first, -1), send_x(first, 2), send_x(first, 1)]
    line_b2, line_a2 = send_z(line_b1, 1), send_z(line_a1, -1)
    near_0 = jnp.concatenate([second, line_a1, line_b1, line_a2])
    near_a1, near_b1 = send_x(near_0, -1), send_x(near_0, 1)
    line_b3, line_a3 = send_z(line_b2, 1), send_z(line_a2, -1)
    quad, line_b3, line_a3 = after((jnp.concatenate(quad), line_b3, line_a3))
    quad_b1, quad_a1 = send_z(quad, 1), send_z(quad, -1)
    line_4 = send_z(line_b3, 1)
    cut = near_0.shape[0] // 2
    quad_b2, quad_a2 = send_z(quad_b1, 1), send_z(quad_a1, -1)
    near_b1, near_a1 = after((near_b1, near_a1, quad_b1, quad_a1))[:2]
    near_2 = jnp.concatenate([send_x(near_b1[:cut], 1), send_x(near_a1[cut:], -1)])
    far_0 = jnp.concatenate([line_b2, line_a3, line_b3, line_4])
    far_0, near_2 = after((far_0, near_2))
    far_a1, far_b1 = send_x(far_0, -1), send_x(far_0, 1)
    quad_b3, quad_a3 = send_z(quad_b2, 1), send_z(quad_a2, -1)
    near_2, quad_b2, quad_a2 = after((near_2, quad_b2, quad_a2))
    near_out = expert_list([near_0, near_a1, near_2, near_b1])
    far_2 = jnp.concatenate([send_x(far_b1[:cut], 1), send_x(far_a1[cut:], -1)])
    near_out, quad_a2, quad_b2 = after((near_out, quad_a2, quad_b2))
    quad_out = dict(
        zip((0, 1, 7, 2, 6), expert_list([quad, quad_a1, quad_b1, quad_a2, quad_b2]))
    )
    far_2, quad_b3, quad_a3 = after((far_2, quad_b3, quad_a3))
    far_out = expert_list([far_0, far_a1, far_2, far_b1])
    cut_quad = quad.shape[0] // 2
    quad_4 = jnp.concatenate([send_z(quad_b3[:cut_quad], 1), send_z(quad_a3[cut_quad:], -1)])
    far_came = sum_x_first(far_out)
    quad_out.update(zip((3, 5, 4), expert_list([quad_a3, quad_b3, quad_4])))
    far_sum = sum_x_second(far_out, far_came)
    near_out, far_sum = after((near_out, far_sum))
    near_sum = sum_x_second(near_out, sum_x_first(near_out))
    line_sum = {}
    for order, total in (((0, 1, 7, 2), near_sum), ((6, 3, 5, 4), far_sum)):
        for k, d in enumerate(order):
            line_sum[d] = total[k * size : (k + 1) * size].astype(BF16)
    quad_steps, line_steps = sum_z_steps(quad_out, True), sum_z_steps(line_sum, False)
    quad_came, line_came = next(quad_steps), next(line_steps)
    quad_came = quad_steps.send(quad_came)
    line_came = after((line_came, near_sum))[0]
    for _ in range(2):
        line_came = after((line_came, quad_came))[0]
        quad_came, line_came = quad_steps.send(quad_came), line_steps.send(line_came)
    quad_sum = quad_steps.send(quad_came).astype(BF16)
    line_came = line_steps.send(line_came)
    first_sum = sum_x_direct([quad_sum[k * cut_rows : (k + 1) * cut_rows] for k in range(NX)])
    second_sum = line_steps.send(line_came)

    expert_out = jnp.concatenate([first_sum, second_sum]).astype(BF16)
    returned = lax.all_to_all(expert_out, "exp", split_axis=0, concat_axis=0, tiled=True)
    mixing = jnp.sum(taken.astype(F32) * route_weights[:, :, None], axis=1)
    moe_sum = jnp.dot(mixing, returned.astype(F32), precision=lax.Precision.HIGHEST)
    return ((hidden + moe_sum).astype(BF16), moe_sum)


def solution(mesh):
    in_specs = (
        P("seq", "exp"),
        P("seq", "exp"),
        P(None, "exp"),
        P("exp"),
        P("exp", None),
        P("exp", None),
        P(None, "exp"),
        P("exp"),
        P(None, "exp"),
        P("exp"),
        P("exp", "seq"),
        P(("seq", "exp"), None),
        P(),
        P(),
        P("exp", None, "seq"),
        P("exp", None, "seq"),
        P("exp", "seq", None),
        P(("seq", "exp"), None),
    )
    out_specs = (P(("seq", "exp"), None), P(("seq", "exp"), None))
    return jax.shard_map(body, mesh=mesh, in_specs=in_specs, out_specs=out_specs, check_vma=False)
```

```python
import jax
import jax.numpy as jnp
from jax import lax
from jax.experimental import pallas as pl
from jax.experimental.pallas import tpu as pltpu
from jax.sharding import PartitionSpec as P

NX = 4
LANES = 128
F32 = jnp.float32
BF16 = jnp.bfloat16


def seq_sizes():
    count = lax.axis_size("seq")
    return count // NX, NX


def groups_x():
    nz, nx = seq_sizes()
    return [[z * nx + x for x in range(nx)] for z in range(nz)]


def groups_z():
    nz, nx = seq_sizes()
    return [[z * nx + x for z in range(nz)] for x in range(nx)]


def send_z(block, step):
    nz, nx = seq_sizes()
    route = [
        (z * nx + x, ((z + step) % nz) * nx + x) for z in range(nz) for x in range(nx)
    ]
    return lax.ppermute(block, "seq", route)


def send_x(block, step):
    nz, nx = seq_sizes()
    route = [(z * nx + x, z * nx + (x + step) % nx) for z in range(nz) for x in range(nx)]
    return lax.ppermute(block, "seq", route)


def padded(block, before, behind):
    return jnp.pad(block.astype(F32), ((before, behind), (0, 0)))


def sum_z_steps(parts, both):
    half = parts[4].shape[0] // 2
    if both:
        came = yield send_z(parts[4][:half], 1), send_z(parts[4][half:], -1)
        came = yield (
            send_z((parts[3] + padded(came[0], 0, half)).astype(BF16), 1),
            send_z((parts[5] + padded(came[1], half, 0)).astype(BF16), -1),
        )
    else:
        came = yield (send_z(parts[4], 1),)
        came, below = lax.optimization_barrier((came, parts[5]))
        came = yield (
            send_z((parts[3] + came[0].astype(F32)).astype(BF16), 1),
            send_z(below, -1),
        )
    for up, down in ((2, 6), (1, 7)):
        came = yield (
            send_z((parts[up] + came[0].astype(F32)).astype(BF16), 1),
            send_z((parts[down] + came[1].astype(F32)).astype(BF16), -1),
        )
    yield parts[0] + came[0].astype(F32) + came[1].astype(F32)


def sum_x_first(parts):
    half = parts[2].shape[0] // 2
    return send_x(parts[2][:half], 1), send_x(parts[2][half:], -1)


def sum_x_second(parts, came):
    half = parts[2].shape[0] // 2
    up = send_x((parts[1] + padded(came[0], 0, half)).astype(BF16), 1)
    down = send_x((parts[3] + padded(came[1], half, 0)).astype(BF16), -1)
    return parts[0] + up.astype(F32) + down.astype(F32)


def sum_x_direct(parts):
    came = [send_x(parts[1], 1), send_x(parts[2], 2), send_x(parts[3], -1)]
    total = parts[0].astype(F32)
    for part in came:
        total = total + part.astype(F32)
    return total


def scan_kernel(
    low_ref, weight_ref, bias_ref, rates_ref, act_ref, maps_ref, out_ref, passed_ref, ends_ref,
    delta_ref, driven_ref,
):
    rows, width = act_ref.shape
    states = rates_ref.shape[0]
    tiles = width // LANES
    raw = jnp.dot(low_ref[...], weight_ref[...], preferred_element_type=F32) + bias_ref[...]
    delta = jnp.maximum(raw, 0.0) + jnp.log1p(jnp.exp(-jnp.abs(raw)))
    delta_ref[...] = delta
    driven_ref[...] = delta * act_ref[...].astype(F32)
    rate = -jnp.exp(rates_ref[...])

    def step(t, carry):
        state, passed = carry
        delta_t = delta_ref[pl.ds(t, 1), :]
        driven_t = driven_ref[pl.ds(t, 1), :]
        maps_t = maps_ref[t]
        input_t = jnp.concatenate([maps_t[:states]] * tiles, axis=1)
        output_t = jnp.concatenate([maps_t[states:]] * tiles, axis=1)
        state = jnp.exp(delta_t * rate) * state + driven_t * input_t
        passed = passed + delta_t
        out_ref[pl.ds(t, 1), :] = jnp.sum(output_t * state, axis=0, keepdims=True)
        passed_ref[pl.ds(t, 1), :] = passed
        return state, passed

    state, passed = lax.fori_loop(
        0, rows, step, (jnp.zeros((states, width), F32), jnp.zeros((1, width), F32)), unroll=4
    )
    ends_ref[:states, :] = state
    ends_ref[states:, :] = passed


def finish_kernel(
    local_ref, passed_ref, start_ref, rates_ref, maps_ref, act_ref, skip_ref, gate_ref, gated_ref,
    full_ref,
):
    rows, width = act_ref.shape
    states = rates_ref.shape[0]
    tiles = width // LANES
    rate = -jnp.exp(rates_ref[...])
    start = start_ref[...]

    def step(t, carry):
        left = jnp.exp(passed_ref[pl.ds(t, 1), :] * rate) * start
        output_t = jnp.concatenate([maps_ref[t][states:]] * tiles, axis=1)
        full_ref[pl.ds(t, 1), :] = local_ref[pl.ds(t, 1), :] + jnp.sum(
            output_t * left, axis=0, keepdims=True
        )
        return carry

    lax.fori_loop(0, rows, step, 0, unroll=4)
    gate = gate_ref[...].astype(F32)
    scan_out = full_ref[...] + skip_ref[...] * act_ref[...].astype(F32)
    gated_ref[...] = (scan_out * (gate / (1.0 + jnp.exp(-gate)))).astype(BF16)


VMEM = pl.BlockSpec(memory_space=pltpu.VMEM)


def local_scan(low, weight, bias, rates, act, maps):
    rows, width = act.shape
    return pl.pallas_call(
        scan_kernel,
        out_shape=(
            jax.ShapeDtypeStruct((rows, width), F32),
            jax.ShapeDtypeStruct((rows, width), F32),
            jax.ShapeDtypeStruct((rates.shape[0] + 1, width), F32),
        ),
        in_specs=[VMEM] * 6,
        out_specs=(VMEM,) * 3,
        scratch_shapes=[pltpu.VMEM((rows, width), F32), pltpu.VMEM((rows, width), F32)],
        compiler_params=pltpu.CompilerParams(vmem_limit_bytes=16 * 2**20),
    )(low, weight, bias, rates, act, maps)


def finish_scan(local, passed, start, rates, maps, act, skip, gate):
    rows, width = act.shape
    return pl.pallas_call(
        finish_kernel,
        out_shape=jax.ShapeDtypeStruct((rows, width), BF16),
        in_specs=[VMEM] * 8,
        out_specs=VMEM,
        scratch_shapes=[pltpu.VMEM((rows, width), F32)],
        compiler_params=pltpu.CompilerParams(vmem_limit_bytes=16 * 2**20),
    )(local, passed, start, rates, maps, act, skip, gate)


def expert_kernel(count, steps, *refs):
    rows = refs[:count]
    gate_ref, up_ref, down_ref = refs[count : count + 3]
    outs = refs[count + 3 : 2 * count + 3]
    gate_sum, up_sum, act_ref = refs[2 * count + 3 :]
    size = rows[0].shape[0]
    i = pl.program_id(0)

    @pl.when(i < steps)
    def _():
        taken = jnp.concatenate([r[...] for r in rows], axis=0)
        across = (((1,), (1,)), ((), ()))
        gate = lax.dot_general(taken, gate_ref[...], across, preferred_element_type=F32)
        up = lax.dot_general(taken, up_ref[...], across, preferred_element_type=F32)

        @pl.when(i == 0)
        def _():
            gate_sum[...] = gate
            up_sum[...] = up

        @pl.when(i > 0)
        def _():
            gate_sum[...] += gate
            up_sum[...] += up

    @pl.when(i >= steps)
    def _():
        @pl.when(i == steps)
        def _():
            gate = gate_sum[...]
            act_ref[...] = (gate / (1.0 + jnp.exp(-gate)) * up_sum[...]).astype(BF16)

        out = jnp.dot(act_ref[...], down_ref[...], preferred_element_type=F32).astype(BF16)
        for k in range(count):
            outs[k][...] = out[k * size : (k + 1) * size]


def experts_of(blocks, gate_local, up_local, down_local):
    count = len(blocks)
    size, features = blocks[0].shape
    hidden = gate_local.shape[0]
    steps = 2
    width = features // steps
    early = lambda i: jnp.minimum(i, steps - 1)
    late = lambda i: jnp.maximum(i - steps, 0)
    flops = 6 * count * size * features * hidden
    moved = 6 * features * hidden + 4 * count * size * features
    return pl.pallas_call(
        lambda *refs: expert_kernel(count, steps, *refs),
        grid=(2 * steps,),
        out_shape=[jax.ShapeDtypeStruct((size, features), BF16)] * count,
        in_specs=[pl.BlockSpec((size, width), lambda i: (0, early(i)))] * count
        + [pl.BlockSpec((hidden, width), lambda i: (0, early(i)))] * 2
        + [pl.BlockSpec((hidden, width), lambda i: (0, late(i)))],
        out_specs=[pl.BlockSpec((size, width), lambda i: (0, late(i)))] * count,
        scratch_shapes=[
            pltpu.VMEM((count * size, hidden), F32),
            pltpu.VMEM((count * size, hidden), F32),
            pltpu.VMEM((count * size, hidden), BF16),
        ],
        cost_estimate=pl.CostEstimate(
            flops=flops, bytes_accessed=moved, transcendentals=count * size * hidden
        ),
        compiler_params=pltpu.CompilerParams(vmem_limit_bytes=36 * 2**20),
    )(*blocks, gate_local, up_local, down_local)


def exchanged(blocks, group):
    return lax.all_to_all(
        blocks, "seq", split_axis=0, concat_axis=0, tiled=True, axis_index_groups=group
    )


def after(ends, took, state, rate):
    return jnp.exp(-took * rate) * state + ends


def entering(ends, log_rates):
    nz, nx = seq_sizes()
    states, width = log_rates.shape
    share = width // nx
    z, x = lax.axis_index("seq") // nx, lax.axis_index("seq") % nx
    rate = jnp.exp(lax.dynamic_slice_in_dim(log_rates, x * share, share, axis=1))
    shares = ends.reshape(states + 1, nx, share).transpose(1, 0, 2)
    row = exchanged(shares, groups_x())
    state, took = jnp.zeros(rate.shape, F32), jnp.zeros((1, share), F32)
    for k in range(nx):
        state = after(row[k, :states], row[k, states:], state, rate)
        took = took + row[k, states:]
    total = jnp.concatenate([state, took])
    rows = exchanged(jnp.broadcast_to(total[None], (nz, *total.shape)), groups_z())
    state = jnp.zeros(rate.shape, F32)
    for k in range(nz - 1):
        state = jnp.where(k < z, after(rows[k, :states], rows[k, states:], state, rate), state)
    starts = [state]
    for k in range(nx - 1):
        starts.append(after(row[k, :states], row[k, states:], starts[-1], rate))
    return exchanged(jnp.stack(starts), groups_x()).transpose(1, 0, 2).reshape(states, width)


def mixer(
    mixer_input, gate_input, conv_weight, conv_bias, rank_weight, state_weight, delta_weight,
    delta_bias, log_rates, skip_gain, out_proj,
):
    taps = conv_weight.shape[0]
    block_rows = mixer_input.shape[0]
    nz, nx = seq_sizes()
    experts = lax.axis_size("exp")
    columns = lax.all_gather(
        out_proj, "seq", axis=1, tiled=True, axis_index_groups=groups_z()
    )
    rim_rows = lax.ppermute(
        mixer_input[block_rows - (taps - 1) :], "seq", [(i, i + 1) for i in range(nz * nx - 1)]
    )
    before = jnp.concatenate([rim_rows, mixer_input], axis=0)
    conv_sum = jnp.zeros(mixer_input.shape, F32) + conv_bias[None, :]
    for offset in range(taps):
        conv_sum = conv_sum + conv_weight[offset].astype(F32)[None, :] * before[
            offset : offset + block_rows
        ].astype(F32)
    conv_act = jax.nn.silu(conv_sum).astype(BF16)
    both = jnp.concatenate([rank_weight, state_weight], axis=1)
    sums = jnp.dot(conv_act, both, preferred_element_type=F32)
    rank = rank_weight.shape[1]
    coarse = lax.reduce_precision(sums, 8, 7)
    fine = sums[:, rank:] - coarse[:, rank:]
    sent = jnp.concatenate([coarse, fine], axis=1).astype(BF16)
    summed = jnp.sum(lax.all_gather(sent, "exp").astype(F32), axis=0)
    maps = summed[:, rank : sums.shape[1]] + summed[:, sums.shape[1] :]
    delta_low = summed[:, :rank].astype(BF16)
    wide_maps = jnp.broadcast_to(maps[:, :, None], (*maps.shape, LANES))
    local, passed, ends = local_scan(
        delta_low, delta_weight, delta_bias[None], log_rates, conv_act, wide_maps
    )
    start = entering(ends, log_rates)
    gated = finish_scan(
        local, passed, start, log_rates, wide_maps, conv_act, skip_gain[None], gate_input
    )
    gated_row = lax.all_gather(gated, "seq", axis=0, tiled=True, axis_index_groups=groups_x())
    partial_value = jnp.dot(gated_row, columns, preferred_element_type=F32).astype(BF16)
    planes = [
        [(k * nx + i) * experts + e for i in range(nx) for e in range(experts)] for k in range(nz)
    ]
    came = lax.all_to_all(
        partial_value, ("seq", "exp"), split_axis=0, concat_axis=0, tiled=True,
        axis_index_groups=planes,
    )
    own_rows = block_rows // experts
    came = came.reshape(nx, experts, own_rows, nz, -1).astype(F32)
    return jnp.sum(came, axis=1).transpose(1, 2, 0, 3).reshape(own_rows, -1)


def body(
    mixer_input,
    gate_input,
    conv_weight,
    conv_bias,
    rank_weight,
    state_weight,
    delta_weight,
    delta_bias,
    log_rates,
    skip_gain,
    out_proj,
    residual,
    norm_gain,
    router,
    w_gate,
    w_up,
    w_down,
    routes,
):
    mamba_out = mixer(
        mixer_input, gate_input, conv_weight, conv_bias, rank_weight, state_weight,
        delta_weight, delta_bias, log_rates, skip_gain, out_proj,
    )
    tok_dev = residual.shape[0]
    hidden = residual.astype(F32) + mamba_out
    mean_square = jnp.mean(hidden * hidden, axis=1, keepdims=True)
    normed = (hidden * lax.rsqrt(mean_square + 1e-05) * norm_gain[None, :]).astype(BF16)
    logits = jnp.dot(normed.astype(F32), router, precision=lax.Precision.HIGHEST)
    experts = router.shape[1]
    expert_ids = jnp.arange(experts, dtype=jnp.int32)
    matches = (routes[:, :, None] == expert_ids[None, None, :]).astype(F32)
    chosen = jnp.sum(matches * logits[:, None, :], axis=2)
    route_weights = jax.nn.sigmoid(chosen - chosen[:, ::-1])
    capacity = max(2, 4 * tok_dev // experts)
    flat_ids = routes.reshape(-1)
    route_pos = jnp.arange(flat_ids.shape[0], dtype=jnp.int32)
    earlier_same = (flat_ids[:, None] == flat_ids[None, :]) & (
        route_pos[None, :] < route_pos[:, None]
    )
    slot_rank = jnp.sum(earlier_same.astype(jnp.int32), axis=1)
    slot_of = (flat_ids * capacity + slot_rank).reshape(tok_dev, 2)
    slot_ids = jnp.arange(experts * capacity, dtype=jnp.int32)
    taken = slot_of[:, :, None] == slot_ids[None, None, :]
    placing = jnp.sum(taken.astype(F32), axis=1).astype(BF16)
    outbound = lax.dot_general(
        placing, normed, (((0,), (0,)), ((), ())), preferred_element_type=F32
    ).astype(BF16)
    arrived = lax.all_to_all(outbound, "exp", split_axis=0, concat_axis=0, tiled=True)
    gate_local, up_local, down_local = w_gate[0].T, w_up[0].T, w_down[0]

    def expert_list(blocks):
        return experts_of(blocks, gate_local, up_local, down_local)

    cut_rows = arrived.shape[0] // 2
    first, second = arrived[:cut_rows], arrived[cut_rows:]
    size = second.shape[0]
    after = lax.optimization_barrier
    line_b1, line_a1 = send_z(second, 1), send_z(second, -1)
    quad = [first, send_x(first, -1), send_x(first, 2), send_x(first, 1)]
    line_b2, line_a2 = send_z(line_b1, 1), send_z(line_a1, -1)
    near_0 = jnp.concatenate([second, line_a1, line_b1, line_a2])
    near_a1, near_b1 = send_x(near_0, -1), send_x(near_0, 1)
    line_b3, line_a3 = send_z(line_b2, 1), send_z(line_a2, -1)
    quad, line_b3, line_a3 = after((jnp.concatenate(quad), line_b3, line_a3))
    quad_b1, quad_a1 = send_z(quad, 1), send_z(quad, -1)
    line_4 = send_z(line_b3, 1)
    own_quad, own_near = expert_list([quad, near_0])
    line_4, own_near = after((line_4, own_near))
    cut = near_0.shape[0] // 2
    quad_b2, quad_a2 = send_z(quad_b1, 1), send_z(quad_a1, -1)
    near_b1, near_a1 = after((near_b1, near_a1, quad_b1, quad_a1))[:2]
    near_2 = jnp.concatenate([send_x(near_b1[:cut], 1), send_x(near_a1[cut:], -1)])
    far_0 = jnp.concatenate([line_b2, line_a3, line_b3, line_4])
    far_0, near_2 = after((far_0, near_2))
    far_a1, far_b1 = send_x(far_0, -1), send_x(far_0, 1)
    quad_b3, quad_a3 = send_z(quad_b2, 1), send_z(quad_a2, -1)
    near_2, quad_b2, quad_a2 = after((near_2, quad_b2, quad_a2))
    near_out = [own_near, *expert_list([near_a1, near_2, near_b1])]
    far_2 = jnp.concatenate([send_x(far_b1[:cut], 1), send_x(far_a1[cut:], -1)])
    near_out, quad_a2, quad_b2 = after((near_out, quad_a2, quad_b2))
    quad_out = dict(zip((1, 7, 2, 6), expert_list([quad_a1, quad_b1, quad_a2, quad_b2])))
    quad_out[0] = own_quad
    far_2, quad_b3, quad_a3 = after((far_2, quad_b3, quad_a3))
    far_out = expert_list([far_0, far_a1, far_2, far_b1])
    cut_quad = quad.shape[0] // 2
    quad_4 = jnp.concatenate([send_z(quad_b3[:cut_quad], 1), send_z(quad_a3[cut_quad:], -1)])
    far_came = sum_x_first(far_out)
    quad_out.update(zip((3, 5, 4), expert_list([quad_a3, quad_b3, quad_4])))
    far_sum = sum_x_second(far_out, far_came)
    near_out, far_sum = after((near_out, far_sum))
    near_sum = sum_x_second(near_out, sum_x_first(near_out))
    line_sum = {}
    for order, total in (((0, 1, 7, 2), near_sum), ((6, 3, 5, 4), far_sum)):
        for k, d in enumerate(order):
            line_sum[d] = total[k * size : (k + 1) * size].astype(BF16)
    quad_steps, line_steps = sum_z_steps(quad_out, True), sum_z_steps(line_sum, False)
    quad_came, line_came = next(quad_steps), next(line_steps)
    quad_came = quad_steps.send(after(quad_came))
    line_came = after((line_came, near_sum))[0]
    for _ in range(2):
        quad_came = after(quad_came)
        line_came = after((line_came, quad_came))[0]
        quad_came, line_came = quad_steps.send(quad_came), line_steps.send(line_came)
    quad_sum = quad_steps.send(quad_came).astype(BF16)
    line_came = line_steps.send(line_came)
    first_sum = sum_x_direct([quad_sum[k * cut_rows : (k + 1) * cut_rows] for k in range(NX)])
    second_sum = line_steps.send(line_came)

    expert_out = jnp.concatenate([first_sum, second_sum]).astype(BF16)
    returned = lax.all_to_all(expert_out, "exp", split_axis=0, concat_axis=0, tiled=True)
    mixing = jnp.sum(taken.astype(F32) * route_weights[:, :, None], axis=1)
    moe_sum = jnp.dot(mixing, returned.astype(F32), precision=lax.Precision.HIGHEST)
    return ((hidden + moe_sum).astype(BF16), moe_sum)


def solution(mesh):
    in_specs = (
        P("seq", "exp"),
        P("seq", "exp"),
        P(None, "exp"),
        P("exp"),
        P("exp", None),
        P("exp", None),
        P(None, "exp"),
        P("exp"),
        P(None, "exp"),
        P("exp"),
        P("exp", "seq"),
        P(("seq", "exp"), None),
        P(),
        P(),
        P("exp", None, "seq"),
        P("exp", None, "seq"),
        P("exp", "seq", None),
        P(("seq", "exp"), None),
    )
    out_specs = (P(("seq", "exp"), None), P(("seq", "exp"), None))
    return jax.shard_map(body, mesh=mesh, in_specs=in_specs, out_specs=out_specs, check_vma=False)
```
